512 devices in a mesh: gz: 32 (over y_hi, z), gy: 16 (over y_lo, x, core).
Axes of the slice: x: 4, y: 4 (y_hi: 2, y_lo: 2; y = y_hi * 2 + y_lo), z: 16, core: 2. Of those that a mesh axis runs over, the one named last changes fastest.
Arguments:
- observed: float32 [128, 512, 1024], P('gz', 'gy'), may hold values from 0.15 to 6.5
- estimate: float32 [128, 512, 1024], P('gz', 'gy'), may hold values from 0.35 to 2.6
- psf_lateral: float32 [31], replicated, may hold values from 0.1 to 1
- psf_axial: float32 [129], replicated, may hold values from 0.05 to 1
Outputs:
- restored: float32 [128, 512, 1024], P('gz', 'gy')
The draws below stay inside these ranges and needn't reach their ends.
All inputs are finite; a program needn't handle non-finite values.
Results may differ from the reference program's by a relative error of at most 0.0003.
Values sent between devices are 32-bit elements; how exact they have to be, the bound alone decides.
No kernel may reach another device: no remote copies, remote signals or barrier semaphores. Data moves between devices by JAX's collectives and lax.ppermute only.
A program may use at most 64 MiB of HBM per device.

```python
import math
import jax
import jax.numpy as jnp
from jax import lax

NX = 1024
ITERS = 2
LAT_TAPS = 31
AX_TAPS = 129
NZ = 128
NY = 512


def grid_positions():
    plane_pos = jnp.arange(NZ, dtype=jnp.float32).reshape(NZ, 1, 1)
    row_pos = jnp.arange(NY, dtype=jnp.float32).reshape(1, NY, 1)
    column_pos = jnp.arange(NX, dtype=jnp.float32).reshape(1, 1, NX)
    return (plane_pos, row_pos, column_pos)


def signed_rate(key, count, shortest, longest):
    first, second = jax.random.split(key)
    rate = jnp.exp(jax.random.uniform(first, (count,), jnp.float32, math.log(1.0 / longest), math.log(1.0 / shortest)))
    signs = jnp.where(jax.random.uniform(second, (count,), jnp.float32) < 0.5, -1.0, 1.0)
    return rate * signs


def wave_params(key, count):
    keys = jax.random.split(key, 5)
    wave_z = signed_rate(keys[0], count, 128.0, 512.0)
    wave_y = signed_rate(keys[1], count, 40.0, 200.0)
    wave_x = signed_rate(keys[2], count, 40.0, 200.0)
    phase = jax.random.uniform(keys[3], (count,), jnp.float32, 0.0, 2.0 * math.pi)
    weight = jax.random.uniform(keys[4], (count,), jnp.float32, 0.5, 1.0)
    return (wave_z, wave_y, wave_x, phase, weight)


def wave_angle(params, component):
    wave_z, wave_y, wave_x, phase, weight = params
    plane_pos, row_pos, column_pos = grid_positions()
    linear = wave_z[component] * plane_pos + wave_y[component] * row_pos + wave_x[component] * column_pos
    return 2.0 * math.pi * linear + phase[component]


def wave_sum(key):
    params = wave_params(key, 4)
    total = jnp.zeros((NZ, NY, NX), jnp.float32)
    for component in range(4):
        total = total + params[4][component] * jnp.sin(wave_angle(params, component))
    return total / jnp.sum(params[4])


def draw_observed(key, part):
    field_key = jax.random.fold_in(key, 11)
    noise_key = jax.random.fold_in(key, 12)
    field = wave_sum(field_key)
    noise = jnp.exp(jax.random.uniform(noise_key, (NZ, NY, NX), jnp.float32, math.log(0.5), math.log(2.0)))
    return (jnp.exp(1.1 * field) * noise).astype(jnp.float32)


def draw_estimate(key, part):
    field_key = jax.random.fold_in(key, 21)
    noise_key = jax.random.fold_in(key, 22)
    field = wave_sum(field_key)
    noise = jnp.exp(jax.random.uniform(noise_key, (NZ, NY, NX), jnp.float32, math.log(0.7), math.log(1.4)))
    return (jnp.exp(0.6 * field) * noise).astype(jnp.float32)


def setup_inputs(seed: int = 0) -> dict:
    streams_of = jax.random.split(jax.random.key(seed), 5)
    observed = draw_observed(jax.random.fold_in(streams_of[4], 71), 0)
    estimate = draw_estimate(jax.random.fold_in(streams_of[4], 71), 0)
    psf_lateral = jnp.clip(jnp.exp(jax.random.uniform(streams_of[2], (LAT_TAPS,), jnp.float32, math.log(0.1), math.log(1.0))), 0.1, 1.0)
    psf_axial = jnp.clip(jnp.exp(jax.random.uniform(streams_of[3], (AX_TAPS,), jnp.float32, math.log(0.05), math.log(1.0))), 0.05, 1.0)
    return {"observed": observed, "estimate": estimate, "psf_lateral": psf_lateral, "psf_axial": psf_axial}


def axial_matrix(weights, planes):
    radius = (weights.shape[0] - 1) // 2
    padded = jnp.pad(weights, (planes, planes))

    def one_row(plane):
        return lax.dynamic_slice(padded, ((radius + planes - plane).astype(jnp.int32),), (planes,))

    return jax.vmap(one_row)(jnp.arange(planes, dtype=jnp.int32))


def lateral(volume, weights):
    radius = (weights.shape[0] - 1) // 2
    rows_y = volume.shape[1]
    cols_x = volume.shape[2]
    padded = jnp.pad(volume, ((0, 0), (radius, radius), (0, 0)))
    summed = jnp.zeros(volume.shape, volume.dtype)
    for tap in range(weights.shape[0]):
        summed = summed + weights[tap] * padded[:, tap:tap + rows_y, :]
    padded = jnp.pad(summed, ((0, 0), (0, 0), (radius, radius)))
    result = jnp.zeros(volume.shape, volume.dtype)
    for tap in range(weights.shape[0]):
        result = result + weights[tap] * padded[:, :, tap:tap + cols_x]
    return result


def axial(volume, matrix):
    planes = volume.shape[0]
    flat = jnp.dot(matrix, volume.reshape(planes, -1), precision=lax.Precision.HIGHEST)
    return flat.reshape(volume.shape)


def reference(observed, estimate, psf_lateral, psf_axial):
    lateral_taps = psf_lateral / jnp.sum(psf_lateral)
    axial_taps = psf_axial / jnp.sum(psf_axial)
    flipped = lateral_taps[::-1]
    matrix = axial_matrix(axial_taps, observed.shape[0])
    back_matrix = matrix.T
    current = estimate
    for step in range(ITERS):
        blurred = axial(lateral(current, lateral_taps), matrix)
        quotient = observed / blurred
        correction = lateral(axial(quotient, back_matrix), flipped)
        current = current * correction
    return current
```

```python
import functools
import jax
import jax.numpy as jnp
from jax import lax
from jax.experimental import pallas as pl
from jax.experimental.pallas import tpu as pltpu
from jax.sharding import PartitionSpec as P

ITERS = 2
F32 = jnp.float32
BF16 = jnp.bfloat16
H = 15
G = 64
T = 32
HALF = T // 2
NX = 1024
TILES = NX // T
NZ = 128
TILE = (T, T, NZ)
PART = (HALF, T, NZ)

VMEM = pl.BlockSpec(memory_space=pltpu.VMEM)
SMEM = pl.BlockSpec(memory_space=pltpu.SMEM)


def call(body, outs, operands, smem=(), flops=4_000_000, moved=2_000_000, scratch=()):
    return pl.pallas_call(
        body,
        out_shape=[jax.ShapeDtypeStruct(s, d) for s, d in outs],
        in_specs=[SMEM if i in smem else VMEM for i in range(len(operands))],
        out_specs=[VMEM] * len(outs),
        scratch_shapes=list(scratch),
        cost_estimate=pl.CostEstimate(flops=flops, bytes_accessed=moved, transcendentals=0),
        compiler_params=pltpu.CompilerParams(vmem_limit_bytes=24 * 1024 * 1024),
    )(*operands)


def split(v):
    hi = v.astype(BF16)
    return hi, (v - hi.astype(F32)).astype(BF16)


def swap_groups(rows):
    lane = lax.broadcasted_iota(jnp.int32, rows[0].shape, 1)
    low64, low32 = lane < 64, (lane & 32) == 0
    a, b, c, d = rows
    a, c = jnp.where(low64, a, pltpu.roll(c, 64, 1)), jnp.where(low64, pltpu.roll(a, 64, 1), c)
    b, d = jnp.where(low64, b, pltpu.roll(d, 64, 1)), jnp.where(low64, pltpu.roll(b, 64, 1), d)
    a, b = jnp.where(low32, a, pltpu.roll(b, 32, 1)), jnp.where(low32, pltpu.roll(a, 96, 1), b)
    c, d = jnp.where(low32, c, pltpu.roll(d, 32, 1)), jnp.where(low32, pltpu.roll(c, 96, 1), d)
    return a, b, c, d


def to_tiles_kernel(block_ref, out_ref):
    for z in range(4):
        for th in range(8):
            rows = [block_ref[z, pl.ds(8 * yh, 8), pl.ds(128 * th, 128)] for yh in range(4)]
            for tl, tile in enumerate(swap_groups(rows)):
                out_ref[4 * th + tl, z] = tile


def to_tiles_shifted_kernel(shift_ref, block_ref, out_ref, rolled):
    for z in range(4):
        rolled[z] = pltpu.roll(block_ref[z], shift_ref[0], 1)
    to_tiles_kernel(rolled, out_ref)


def from_tiles_kernel(tiles_ref, out_ref):
    for z in range(4):
        for th in range(8):
            tiles = [tiles_ref[4 * th + tl, z] for tl in range(4)]
            for yh, row in enumerate(swap_groups(tiles)):
                out_ref[z, pl.ds(8 * yh, 8), pl.ds(128 * th, 128)] = row


def matrices_kernel(place_ref, lat_ref, band_ref, z_fwd, z_bwd, x_fwd, x_bwd):
    tile, side = place_ref[0], place_ref[1]
    band = band_ref[...]
    band = band / jnp.sum(band)
    wide = jnp.broadcast_to(band, (NZ, 2 * NZ))
    back = pltpu.roll(wide, 0, 1, stride=1, stride_axis=0)[:, :NZ]
    for m, ref in ((back.T, z_fwd), (back, z_bwd)):
        hi, lo = split(m)
        ref[pl.ds(0, NZ), pl.ds(0, NZ)] = hi
        ref[pl.ds(NZ, NZ), pl.ds(0, NZ)] = hi
        ref[pl.ds(0, NZ), pl.ds(NZ, NZ)] = lo
        ref[pl.ds(NZ, NZ), pl.ds(NZ, NZ)] = jnp.zeros_like(lo)
    total = lat_ref[0]
    for k in range(1, 2 * H + 1):
        total = total + lat_ref[k]
    row = lax.broadcasted_iota(jnp.int32, (T, NZ), 0)
    lane = lax.broadcasted_iota(jnp.int32, (T, NZ), 1)
    own, first = lane < 64, (lane & 32) == 0
    col = lane & 31
    here = T * tile
    shifted = here + H * side
    wrap = lambda v: v & (NX - 1)
    src_f = wrap(jnp.where(own, here, here + T * side) + col)
    dst_f = wrap(shifted + row)
    src_b = wrap(jnp.where(own, shifted, shifted - T * side) + col)
    dst_b = wrap(here + row)
    for d, ref in ((src_f - dst_f, x_fwd), (dst_b - src_b, x_bwd)):
        m = jnp.zeros((T, NZ), F32)
        for k in range(2 * H + 1):
            m = jnp.where(d == k - H, lat_ref[k], m)
        scale = jnp.full((T, NZ), total, F32)
        m = m / scale / scale
        hi, lo = split(m)
        ref[pl.ds(0, T), :] = hi
        ref[pl.ds(T, T), :] = jnp.where(first, lo.astype(F32), 0.0).astype(BF16)


def z_pass(v, m):
    r = jnp.dot(jnp.concatenate(split(v), axis=1), m, preferred_element_type=F32)
    return r[:, :NZ] + r[:, NZ:]


def x_pass(own, nbr, m):
    columns = []
    for o, n in zip(own, nbr):
        columns.append(jnp.concatenate([*split(o), *split(n)], axis=0))
    r = jnp.dot(m, jnp.concatenate(columns, axis=1), preferred_element_type=F32)
    r = r[:T] + r[T:]
    return [r[:, NZ * i : NZ * (i + 1)] for i in range(len(own))]


def y_pass(parts, taps_ref, flip, emit):
    def source(e, x8):
        part, r = divmod(e + 1, HALF)
        return parts[part][r, pl.ds(x8, 8), :]

    taps = [taps_ref[2 * H - k if flip else k] for k in range(2 * H + 1)]

    @pl.loop(0, T // 8)
    def _(i):
        x8 = pl.multiple_of(i * 8, 8)
        for y0 in range(0, T, 8):
            acc = [None] * 8
            for e in range(8 + 2 * H):
                v = source(y0 + e, x8)
                for j in range(max(0, e - 2 * H), min(8, e + 1)):
                    term = taps[e - j] * v
                    acc[j] = term if acc[j] is None else acc[j] + term
            for j in range(8):
                emit(y0 + j, x8, acc[j])


def half(y, first, second):
    return (first, y) if y < HALF else (second, y - HALF)


def arrive_kernel(tiles_ref, m_ref, cur_ref, a_ref, b_ref):
    m = m_ref[...]
    for lo in range(8):
        v = tiles_ref[pl.ds(lo, NZ, stride=8), :].T
        w = z_pass(v, m)
        for hi in range(4):
            y = 8 * hi + lo
            cur_ref[y] = v[T * hi : T * (hi + 1)]
            ref, r = half(y, a_ref, b_ref)
            ref[r] = w[T * hi : T * (hi + 1)]


def arrive_plain_kernel(tiles_ref, out_ref):
    for lo in range(8):
        v = tiles_ref[pl.ds(lo, NZ, stride=8), :].T
        for hi in range(4):
            out_ref[8 * hi + lo] = v[T * hi : T * (hi + 1)]


def y_kernel(taps_ref, up, first, second, down, out_ref):
    def emit(y, x8, v):
        out_ref[y, pl.ds(x8, 8), :] = v

    y_pass((up, first, second, down), taps_ref, False, emit)


def quotient_kernel(own_ref, nbr_ref, obs_ref, m_ref, q_ref):
    m = m_ref[...]
    for y in range(0, T, 2):
        pair = (y, y + 1)
        for i, r in zip(pair, x_pass([own_ref[i] for i in pair], [nbr_ref[i] for i in pair], m)):
            q_ref[i] = obs_ref[i] / r


def back_kernel(own_ref, nbr_ref, mx_ref, mz_ref, a_ref, b_ref):
    mx, mz = mx_ref[...], mz_ref[...]
    for y in range(0, T, 4):
        rows = []
        for i in (y, y + 2):
            pair = (i, i + 1)
            rows += x_pass([own_ref[k] for k in pair], [nbr_ref[k] for k in pair], mx)
        w = z_pass(jnp.concatenate(rows, axis=0), mz)
        for i in range(4):
            ref, r = half(y + i, a_ref, b_ref)
            ref[r] = w[T * i : T * (i + 1)]


def update_kernel(taps_ref, up, first, second, down, cur_ref, m_ref, out_ref, a_ref, b_ref):
    def emit(y, x8, v):
        at = (y, pl.ds(x8, 8), slice(None))
        out_ref[at] = cur_ref[at] * v

    y_pass((up, first, second, down), taps_ref, True, emit)
    m = m_ref[...]
    for y in range(0, T, 4):
        w = z_pass(jnp.concatenate([out_ref[y + i] for i in range(4)], axis=0), m)
        for i in range(4):
            ref, r = half(y + i, a_ref, b_ref)
            ref[r] = w[T * i : T * (i + 1)]


def leave_kernel(taps_ref, up, first, second, down, cur_ref, tiles_ref, work):
    def emit(y, x8, v):
        at = (y, pl.ds(x8, 8), slice(None))
        work[at] = cur_ref[at] * v

    y_pass((up, first, second, down), taps_ref, True, emit)
    for lo in range(8):
        v = jnp.concatenate([work[8 * hi + lo] for hi in range(4)], axis=0)
        tiles_ref[pl.ds(lo, NZ, stride=8), :] = v.T


def local(observed, estimate, psf_lateral, psf_axial):
    n_z, n_y = lax.axis_size("gz"), lax.axis_size("gy")
    gz, gy = lax.axis_index("gz").astype(jnp.int32), lax.axis_index("gy").astype(jnp.int32)
    side = 1 - 2 * (gy % 2)
    joint = ("gz", "gy")

    def turn(sign):
        pairs = []
        for z in range(n_z):
            for y in range(n_y):
                s = sign * (1 if y % 2 == 0 else -1)
                pairs.append(((z + s) % n_z * n_y + y, z * n_y + y))
        return pairs

    ahead, behind = turn(1), turn(-1)
    up = [(i, i + 1) for i in range(n_y - 1)]
    down = [(i + 1, i) for i in range(n_y - 1)]

    def y_parts(first, second):
        return lax.ppermute(second, "gy", up), first, second, lax.ppermute(first, "gy", down)

    def exchange(tiles):
        return lax.all_to_all(tiles, "gz", split_axis=0, concat_axis=0, tiled=True)

    tiles_shape = (TILES, 4, 8, 128)
    flat = (NZ * 8, 128)
    (est_tiles,) = call(to_tiles_kernel, [(tiles_shape, F32)], [estimate])
    shift = jnp.where(side > 0, NX - H, H).astype(jnp.int32).reshape(1)
    (obs_tiles,) = call(
        to_tiles_shifted_kernel,
        [(tiles_shape, F32)],
        [shift, observed],
        smem=(0,),
        scratch=[pltpu.VMEM((4, T, NX), F32)],
    )
    band = jnp.concatenate([psf_axial[G:], jnp.zeros((2 * NZ - 2 * G - 1,), F32), psf_axial[:G]])
    z_fwd, z_bwd, x_fwd, x_bwd = call(
        matrices_kernel,
        [((2 * NZ, 2 * NZ), BF16)] * 2 + [((2 * T, 4 * T), BF16)] * 2,
        [jnp.stack([gz, side]), psf_lateral, band.reshape(1, 2 * NZ)],
        smem=(0, 1),
    )
    est_tiles = exchange(est_tiles)
    obs_tiles = exchange(obs_tiles)
    current, first, second = call(
        arrive_kernel,
        [(TILE, F32), (PART, F32), (PART, F32)],
        [est_tiles.reshape(flat), z_fwd],
    )
    (obs,) = call(arrive_plain_kernel, [(TILE, F32)], [obs_tiles.reshape(flat)])
    for step in range(ITERS):
        (own,) = call(
            y_kernel, [(TILE, F32)], [psf_lateral, *y_parts(first, second)], smem=(0,)
        )
        (own,) = call(
            quotient_kernel, [(TILE, F32)], [own, lax.ppermute(own, joint, ahead), obs, x_fwd]
        )
        first, second = call(
            back_kernel,
            [(PART, F32)] * 2,
            [own, lax.ppermute(own, joint, behind), x_bwd, z_bwd],
        )
        operands = [psf_lateral, *y_parts(first, second), current]
        if step < ITERS - 1:
            current, first, second = call(
                update_kernel,
                [(TILE, F32), (PART, F32), (PART, F32)],
                [*operands, z_fwd],
                smem=(0,),
            )
        else:
            (tiles,) = call(
                leave_kernel, [(flat, F32)], operands, smem=(0,), scratch=[pltpu.VMEM(TILE, F32)]
            )
    tiles = exchange(tiles.reshape(tiles_shape))
    (out,) = call(from_tiles_kernel, [((4, T, NX), F32)], [tiles])
    return out


def solution(mesh):
    in_specs = (P("gz", "gy", None), P("gz", "gy", None), P(), P())
    out_specs = P("gz", "gy", None)
    return jax.shard_map(local, mesh=mesh, in_specs=in_specs, out_specs=out_specs, check_vma=False)
```

```python
import functools
import jax
import jax.numpy as jnp
from jax import lax
from jax.experimental import pallas as pl
from jax.experimental.pallas import tpu as pltpu
from jax.sharding import PartitionSpec as P

ITERS = 2
F32 = jnp.float32
BF16 = jnp.bfloat16
H = 15
TAPS = 2 * H + 1
G = 64
T = 32
HALF = T // 2
NX = 1024
TILES = NX // T
NZ = 128
TILE = (T, T, NZ)

VMEM = pl.BlockSpec(memory_space=pltpu.VMEM)
SMEM = pl.BlockSpec(memory_space=pltpu.SMEM)


def call(body, outs, operands, smem=(), flops=4_000_000, moved=2_000_000, scratch=()):
    return pl.pallas_call(
        body,
        out_shape=[jax.ShapeDtypeStruct(s, d) for s, d in outs],
        in_specs=[SMEM if i in smem else VMEM for i in range(len(operands))],
        out_specs=[VMEM] * len(outs),
        scratch_shapes=list(scratch),
        cost_estimate=pl.CostEstimate(flops=flops, bytes_accessed=moved, transcendentals=0),
        compiler_params=pltpu.CompilerParams(vmem_limit_bytes=24 * 1024 * 1024),
    )(*operands)


def split(v):
    hi = v.astype(BF16)
    return hi, (v - hi.astype(F32)).astype(BF16)


def swap_groups(rows):
    lane = lax.broadcasted_iota(jnp.int32, rows[0].shape, 1)
    low64, low32 = lane < 64, (lane & 32) == 0
    a, b, c, d = rows
    a, c = jnp.where(low64, a, pltpu.roll(c, 64, 1)), jnp.where(low64, pltpu.roll(a, 64, 1), c)
    b, d = jnp.where(low64, b, pltpu.roll(d, 64, 1)), jnp.where(low64, pltpu.roll(b, 64, 1), d)
    a, b = jnp.where(low32, a, pltpu.roll(b, 32, 1)), jnp.where(low32, pltpu.roll(a, 96, 1), b)
    c, d = jnp.where(low32, c, pltpu.roll(d, 32, 1)), jnp.where(low32, pltpu.roll(c, 96, 1), d)
    return a, b, c, d


def tiles_of(read, write):
    for th in range(8):
        rows = [read(pl.ds(8 * yh, 8), pl.ds(128 * th, 128)) for yh in range(4)]
        for tl, tile in enumerate(swap_groups(rows)):
            write(4 * th + tl, tile)


def to_tiles_kernel(block_ref, out_ref):
    def write(t, tile):
        out_ref[t, 0] = tile

    tiles_of(lambda rows, lanes: block_ref[0, rows, lanes], write)


def from_tiles_kernel(tiles_ref, out_ref):
    for th in range(8):
        tiles = [tiles_ref[4 * th + tl, 0] for tl in range(4)]
        for yh, row in enumerate(swap_groups(tiles)):
            out_ref[0, pl.ds(8 * yh, 8), pl.ds(128 * th, 128)] = row


def per_plane(body, out_shape, in_block, out_block, operand):
    def spec(block):
        shape, dim = block
        return pl.BlockSpec(shape, lambda z: tuple(z if d == dim else 0 for d in range(len(shape))))

    return pl.pallas_call(
        body,
        grid=(4,),
        out_shape=jax.ShapeDtypeStruct(out_shape, F32),
        in_specs=[spec(in_block)],
        out_specs=spec(out_block),
        cost_estimate=pl.CostEstimate(flops=1_000_000, bytes_accessed=2_000_000, transcendentals=0),
        compiler_params=pltpu.CompilerParams(vmem_limit_bytes=24 * 1024 * 1024),
    )(operand)


def prepare_kernel(
    place_ref, lat_ref, ax_ref, obs_ref, obs_tiles, z_fwd, z_bwd, x_fwd, x_bwd, y_fwd, y_bwd, rolled
):
    tile, side = place_ref[0], place_ref[1]
    for z in range(4):
        rolled[z] = pltpu.roll(obs_ref[z], place_ref[2], 1)

        def write(t, v, z=z):
            obs_tiles[t, z] = v

        tiles_of(lambda rows, lanes, z=z: rolled[z, rows, lanes], write)
    band = pltpu.roll(ax_ref[...], 2 * NZ - G, 1)
    band = band / jnp.sum(band)
    wide = jnp.broadcast_to(band, (NZ, 2 * NZ))
    back = pltpu.roll(wide, 0, 1, stride=1, stride_axis=0)[:, :NZ]
    for m, ref in ((back.T, z_fwd), (back, z_bwd)):
        hi, lo = split(m)
        ref[pl.ds(0, NZ), pl.ds(0, NZ)] = hi
        ref[pl.ds(NZ, NZ), pl.ds(0, NZ)] = hi
        ref[pl.ds(0, NZ), pl.ds(NZ, NZ)] = lo
        ref[pl.ds(NZ, NZ), pl.ds(NZ, NZ)] = jnp.zeros_like(lo)
    total = lat_ref[0]
    for k in range(TAPS):
        tap = jnp.full((8, NZ), lat_ref[k], F32)
        y_fwd[k] = tap
        y_bwd[TAPS - 1 - k] = tap
        if k > 0:
            total = total + lat_ref[k]
    row = lax.broadcasted_iota(jnp.int32, (T, NZ), 0)
    lane = lax.broadcasted_iota(jnp.int32, (T, NZ), 1)
    own, first = lane < 64, (lane & 32) == 0
    col = lane & 31
    here = T * tile
    shifted = here + H * side
    wrap = lambda v: v & (NX - 1)
    src_f = wrap(jnp.where(own, here, here + T * side) + col)
    dst_f = wrap(shifted + row)
    src_b = wrap(jnp.where(own, shifted, shifted - T * side) + col)
    dst_b = wrap(here + row)
    for d, ref in ((src_f - dst_f, x_fwd), (dst_b - src_b, x_bwd)):
        m = jnp.zeros((T, NZ), F32)
        for k in range(TAPS):
            m = jnp.where(d == k - H, lat_ref[k], m)
        scale = jnp.full((T, NZ), total, F32)
        m = m / scale / scale
        hi, lo = split(m)
        ref[pl.ds(0, T), :] = hi
        ref[pl.ds(T, T), :] = jnp.where(first, lo.astype(F32), 0.0).astype(BF16)


def z_pass(v, m):
    r = jnp.dot(jnp.concatenate(split(v), axis=1), m, preferred_element_type=F32)
    return r[:, :NZ] + r[:, NZ:]


def x_pass(own, nbr, m):
    columns = []
    for o, n in zip(own, nbr):
        columns.append(jnp.concatenate([*split(o), *split(n)], axis=0))
    r = jnp.dot(m, jnp.concatenate(columns, axis=1), preferred_element_type=F32)
    r = r[:T] + r[T:]
    return [r[:, NZ * i : NZ * (i + 1)] for i in range(len(own))]


def y_pass(read, rows, taps_ref, emit):
    taps = [taps_ref[k] for k in range(TAPS)]
    for y0 in range(0, rows, 8):
        acc = [None] * 8
        for e in range(8 + TAPS - 1):
            v = read(y0 + e)
            for j in range(max(0, e - TAPS + 1), min(8, e + 1)):
                term = taps[e - j] * v
                acc[j] = term if acc[j] is None else acc[j] + term
        for j in range(8):
            emit(y0 + j, acc[j])


def rows_of(parts, skip, x8):
    sizes = [p.shape[0] for p in parts]

    def read(e):
        e = e + skip
        for part, size in zip(parts, sizes):
            if e < size:
                return part[e, pl.ds(x8, 8), :]
            e -= size

    return read


def each_x8(body):
    @pl.loop(0, T // 8)
    def _(i):
        body(pl.multiple_of(i * 8, 8))


def z_rows(src_ref, m, out_ref):
    for y in range(0, T, 4):
        w = z_pass(jnp.concatenate([src_ref[y + i] for i in range(4)], axis=0), m)
        for i in range(4):
            out_ref[y + i] = w[T * i : T * (i + 1)]


def arrive_kernel(tiles_ref, out_ref):
    for lo in range(8):
        v = tiles_ref[pl.ds(lo, NZ, stride=8), :].T
        for hi in range(4):
            out_ref[8 * hi + lo] = v[T * hi : T * (hi + 1)]


def blur_kernel(taps_ref, up, cur, down, m_ref, out_ref, work):
    def body(x8):
        def emit(y, v):
            work[y, pl.ds(x8, 8), :] = v

        y_pass(rows_of((up, cur, down), 1, x8), T, taps_ref, emit)

    each_x8(body)
    z_rows(work, m_ref[...], out_ref)


def quotient_kernel(own_ref, nbr_ref, obs_ref, m_ref, q_ref):
    m = m_ref[...]
    for y in range(0, T, 2):
        pair = (y, y + 1)
        for i, r in zip(pair, x_pass([own_ref[i] for i in pair], [nbr_ref[i] for i in pair], m)):
            q_ref[i] = obs_ref[i] / r


def back_kernel(own_ref, nbr_ref, mx_ref, mz_ref, out_ref):
    mx, mz = mx_ref[...], mz_ref[...]
    for y in range(0, T, 4):
        rows = []
        for i in (y, y + 2):
            pair = (i, i + 1)
            rows += x_pass([own_ref[k] for k in pair], [nbr_ref[k] for k in pair], mx)
        w = z_pass(jnp.concatenate(rows, axis=0), mz)
        for i in range(4):
            out_ref[y + i] = w[T * i : T * (i + 1)]


def update_kernel(
    back_ref, fwd_ref, up, own, down, cur_up, cur, cur_down, m_ref, new_ref, out_ref, wide, work
):
    def body(x8):
        at = pl.ds(x8, 8)
        before = rows_of((cur_up, cur, cur_down), 0, x8)

        def emit(r, v):
            v = before(r) * v
            wide[r, at, :] = v
            if HALF <= r < HALF + T:
                new_ref[r - HALF, at, :] = v

        y_pass(rows_of((up, own, down), T - HALF - H, x8), 2 * T, back_ref, emit)

        def emit_blur(y, v):
            work[y, at, :] = v

        y_pass(rows_of((wide,), 1, x8), T, fwd_ref, emit_blur)

    each_x8(body)
    z_rows(work, m_ref[...], out_ref)


def leave_kernel(taps_ref, up, own, down, cur_ref, tiles_ref, work):
    def body(x8):
        def emit(y, v):
            work[y, pl.ds(x8, 8), :] = cur_ref[y, pl.ds(x8, 8), :] * v

        y_pass(rows_of((up, own, down), 1, x8), T, taps_ref, emit)

    each_x8(body)
    for lo in range(8):
        v = jnp.concatenate([work[8 * hi + lo] for hi in range(4)], axis=0)
        tiles_ref[pl.ds(lo, NZ, stride=8), :] = v.T


def local(observed, estimate, psf_lateral, psf_axial):
    n_z, n_y = lax.axis_size("gz"), lax.axis_size("gy")
    gz, gy = lax.axis_index("gz").astype(jnp.int32), lax.axis_index("gy").astype(jnp.int32)
    odd = gy % 2 == 1
    side = 1 - 2 * (gy % 2)
    joint = ("gz", "gy")

    def turn(sign):
        pairs = []
        for z in range(n_z):
            for y in range(n_y):
                s = sign * (1 if y % 2 == 0 else -1)
                pairs.append(((z + s) % n_z * n_y + y, z * n_y + y))
        return pairs

    ahead, behind = turn(1), turn(-1)
    outer = [p for i in range(1, n_y - 1, 2) for p in ((i, i + 1), (i + 1, i))]
    inner = [p for i in range(0, n_y, 2) for p in ((i, i + 1), (i + 1, i))]

    def y_swap(to_outer, to_inner):
        from_outer = lax.ppermute(to_outer, "gy", outer)
        from_inner = lax.ppermute(to_inner, "gy", inner)
        return jnp.where(odd, from_inner, from_outer), jnp.where(odd, from_outer, from_inner)

    def y_halves(v):
        first, second = v[:HALF], v[HALF:]
        return y_swap(jnp.where(odd, second, first), jnp.where(odd, first, second))

    def exchange(tiles):
        return lax.all_to_all(tiles, "gz", split_axis=0, concat_axis=0, tiled=True)

    tiles_shape = (TILES, 4, 8, 128)
    flat = (NZ * 8, 128)
    tile_block = ((TILES, 1, 8, 128), 1)
    row_block = ((1, T, NX), 0)
    est_tiles = per_plane(to_tiles_kernel, tiles_shape, row_block, tile_block, estimate)
    place = jnp.stack([gz, side, jnp.where(odd, H, NX - H).astype(jnp.int32)])
    obs_tiles, z_fwd, z_bwd, x_fwd, x_bwd, y_fwd, y_bwd = call(
        prepare_kernel,
        [(tiles_shape, F32)]
        + [((2 * NZ, 2 * NZ), BF16)] * 2
        + [((2 * T, 4 * T), BF16)] * 2
        + [((TAPS, 8, NZ), F32)] * 2,
        [place, psf_lateral, jnp.pad(psf_axial, (0, 2 * NZ - 2 * G - 1)).reshape(1, 2 * NZ), observed],
        smem=(0, 1),
        scratch=[pltpu.VMEM((4, T, NX), F32)],
    )
    est_tiles = exchange(est_tiles)
    obs_tiles = exchange(obs_tiles)
    (current,) = call(arrive_kernel, [(TILE, F32)], [est_tiles.reshape(flat)])
    (obs,) = call(arrive_kernel, [(TILE, F32)], [obs_tiles.reshape(flat)])
    work = pltpu.VMEM(TILE, F32)
    above, below = y_halves(current)
    (own,) = call(
        blur_kernel, [(TILE, F32)], [y_fwd, above, current, below, z_fwd], scratch=[work]
    )
    for step in range(ITERS):
        (own,) = call(
            quotient_kernel, [(TILE, F32)], [own, lax.ppermute(own, joint, ahead), obs, x_fwd]
        )
        (own,) = call(
            back_kernel, [(TILE, F32)], [own, lax.ppermute(own, joint, behind), x_bwd, z_bwd]
        )
        if step < ITERS - 1:
            up, down = y_swap(own, own)
            current, own = call(
                update_kernel,
                [(TILE, F32)] * 2,
                [y_bwd, y_fwd, up, own, down, above, current, below, z_fwd],
                scratch=[pltpu.VMEM((2 * T, T, NZ), F32), work],
            )
        else:
            up, down = y_halves(own)
            (tiles,) = call(
                leave_kernel, [(flat, F32)], [y_bwd, up, own, down, current], scratch=[work]
            )
    tiles = exchange(tiles.reshape(tiles_shape))
    return per_plane(from_tiles_kernel, (4, T, NX), tile_block, row_block, tiles)


def solution(mesh):
    in_specs = (P("gz", "gy", None), P("gz", "gy", None), P(), P())
    out_specs = P("gz", "gy", None)
    return jax.shard_map(local, mesh=mesh, in_specs=in_specs, out_specs=out_specs, check_vma=False)
```

```python
import functools
import jax
import jax.numpy as jnp
from jax import lax
from jax.experimental import pallas as pl
from jax.experimental.pallas import tpu as pltpu
from jax.sharding import PartitionSpec as P

ITERS = 2
F32 = jnp.float32
BF16 = jnp.bfloat16
H = 15
TAPS = 2 * H + 1
G = 64
T = 32
HALF = T // 2
NX = 1024
TILES = NX // T
NZ = 128

VMEM = pl.BlockSpec(memory_space=pltpu.VMEM)
SMEM = pl.BlockSpec(memory_space=pltpu.SMEM)


def call(body, outs, operands, smem=(), flops=4_000_000, moved=2_000_000, scratch=()):
    return pl.pallas_call(
        body,
        out_shape=[jax.ShapeDtypeStruct(s, d) for s, d in outs],
        in_specs=[SMEM if i in smem else VMEM for i in range(len(operands))],
        out_specs=[VMEM] * len(outs),
        scratch_shapes=list(scratch),
        cost_estimate=pl.CostEstimate(flops=flops, bytes_accessed=moved, transcendentals=0),
        compiler_params=pltpu.CompilerParams(vmem_limit_bytes=24 * 1024 * 1024),
    )(*operands)


def split(v):
    hi = v.astype(BF16)
    return hi, (v - hi.astype(F32)).astype(BF16)


def swap_groups(rows):
    lane = lax.broadcasted_iota(jnp.int32, rows[0].shape, 1)
    low64, low32 = lane < 64, (lane & 32) == 0
    a, b, c, d = rows
    a, c = jnp.where(low64, a, pltpu.roll(c, 64, 1)), jnp.where(low64, pltpu.roll(a, 64, 1), c)
    b, d = jnp.where(low64, b, pltpu.roll(d, 64, 1)), jnp.where(low64, pltpu.roll(b, 64, 1), d)
    a, b = jnp.where(low32, a, pltpu.roll(b, 32, 1)), jnp.where(low32, pltpu.roll(a, 96, 1), b)
    c, d = jnp.where(low32, c, pltpu.roll(d, 32, 1)), jnp.where(low32, pltpu.roll(c, 96, 1), d)
    return a, b, c, d


def tiles_of(read, write):
    for th in range(8):
        rows = [read(pl.ds(8 * yh, 8), pl.ds(128 * th, 128)) for yh in range(4)]
        for tl, tile in enumerate(swap_groups(rows)):
            write(4 * th + tl, tile)


def depart_kernel(block_hbm, tiles_hbm, block, tiles, in_sems, out_sems):
    copies = [pltpu.make_async_copy(block_hbm.at[z], block.at[z], in_sems.at[z]) for z in range(4)]
    for c in copies:
        c.start()
    sent = []
    for z in range(4):
        copies[z].wait()
        for th in range(8):
            rows = [block[z, pl.ds(8 * yh, 8), pl.ds(128 * th, 128)] for yh in range(4)]
            for tl, tile in enumerate(swap_groups(rows)):
                tiles[4 * th + tl, z] = tile
            if z == 3 and th % 2 == 1:
                group = pl.ds(4 * (th - 1), 8)
                sent.append(pltpu.make_async_copy(tiles.at[group], tiles_hbm.at[group], out_sems.at[th // 2]))
                sent[-1].start()
    for c in sent:
        c.wait()


def from_tiles_kernel(tiles_ref, out_ref):
    for th in range(8):
        tiles = [tiles_ref[4 * th + tl, 0] for tl in range(4)]
        for yh, row in enumerate(swap_groups(tiles)):
            out_ref[0, pl.ds(8 * yh, 8), pl.ds(128 * th, 128)] = row


def per_plane(body, out_shape, in_block, out_block, operand):
    def spec(block):
        shape, dim = block
        return pl.BlockSpec(shape, lambda z: tuple(z if d == dim else 0 for d in range(len(shape))))

    return pl.pallas_call(
        body,
        grid=(4,),
        out_shape=jax.ShapeDtypeStruct(out_shape, F32),
        in_specs=[spec(in_block)],
        out_specs=spec(out_block),
        cost_estimate=pl.CostEstimate(flops=1_000_000, bytes_accessed=2_000_000, transcendentals=0),
        compiler_params=pltpu.CompilerParams(vmem_limit_bytes=24 * 1024 * 1024),
    )(operand)


def prepare_kernel(
    place_ref, lat_ref, ax_ref, obs_ref, obs_tiles, z_fwd, z_bwd, x_fwd, x_bwd, y_fwd, y_bwd, y_wide, rolled
):
    tile, side = place_ref[0], place_ref[1]
    for z in range(4):
        rolled[z] = pltpu.roll(obs_ref[z], place_ref[2], 1)

        def write(t, v, z=z):
            obs_tiles[t, z] = v

        tiles_of(lambda rows, lanes, z=z: rolled[z, rows, lanes], write)
    band = pltpu.roll(ax_ref[...], 2 * NZ - G, 1)
    band = band / jnp.sum(band)
    wide = jnp.broadcast_to(band, (NZ, 2 * NZ))
    back = pltpu.roll(wide, 0, 1, stride=1, stride_axis=0)[:, :NZ]
    for m, ref in ((back.T, z_fwd), (back, z_bwd)):
        hi, lo = split(m)
        ref[pl.ds(0, NZ), pl.ds(0, NZ)] = hi
        ref[pl.ds(NZ, NZ), pl.ds(0, NZ)] = hi
        ref[pl.ds(0, NZ), pl.ds(NZ, NZ)] = lo
        ref[pl.ds(NZ, NZ), pl.ds(NZ, NZ)] = jnp.zeros_like(lo)
    total = lat_ref[0]
    for k in range(1, TAPS):
        total = total + lat_ref[k]
    for flip, outs, ins, ref in ((0, T, 2 * T, y_fwd), (1, T, 2 * T, y_bwd), (1, 2 * T, 3 * T, y_wide)):
        row = lax.broadcasted_iota(jnp.int32, (outs, 2 * NZ), 0)
        lane = lax.broadcasted_iota(jnp.int32, (outs, 2 * NZ), 1)
        high = lane < ins
        d = jnp.where(high, lane, lane - ins) - row - 1
        m = jnp.zeros((outs, 2 * NZ), F32)
        for k in range(TAPS):
            m = jnp.where(d == k, lat_ref[TAPS - 1 - k if flip else k], m)
        hi, lo = split(m)
        ref[pl.ds(0, outs), :] = hi[:, : 2 * ins]
        ref[pl.ds(outs, outs), :] = jnp.where(high, lo.astype(F32), 0.0).astype(BF16)[:, : 2 * ins]
    row = lax.broadcasted_iota(jnp.int32, (T, NZ), 0)
    lane = lax.broadcasted_iota(jnp.int32, (T, NZ), 1)
    own, first = lane < 64, (lane & 32) == 0
    col = lane & 31
    here = T * tile
    shifted = here + H * side
    wrap = lambda v: v & (NX - 1)
    src_f = wrap(jnp.where(own, here, here + T * side) + col)
    dst_f = wrap(shifted + row)
    src_b = wrap(jnp.where(own, shifted, shifted - T * side) + col)
    dst_b = wrap(here + row)
    for d, ref in ((src_f - dst_f, x_fwd), (dst_b - src_b, x_bwd)):
        m = jnp.zeros((T, NZ), F32)
        for k in range(TAPS):
            m = jnp.where(d == k - H, lat_ref[k], m)
        scale = jnp.full((T, NZ), total, F32)
        m = m / scale / scale
        hi, lo = split(m)
        ref[pl.ds(0, T), :] = hi
        ref[pl.ds(T, T), :] = jnp.where(first, lo.astype(F32), 0.0).astype(BF16)


def z_pass(v, m):
    r = jnp.dot(jnp.concatenate(split(v), axis=1), m, preferred_element_type=F32)
    return r[:, :NZ] + r[:, NZ:]


def x_pass(own, nbr, m):
    columns = []
    for o, n in zip(own, nbr):
        columns.append(jnp.concatenate([*split(o), *split(n)], axis=0))
    r = jnp.dot(m, jnp.concatenate(columns, axis=1), preferred_element_type=F32)
    r = r[:T] + r[T:]
    return [r[:, NZ * i : NZ * (i + 1)] for i in range(len(own))]


def y_pass(columns, m):
    outs = m.shape[0] // 2
    stacked = [jnp.concatenate(split(c), axis=0) for c in columns]
    r = jnp.dot(m, jnp.concatenate(stacked, axis=1), preferred_element_type=F32)
    return r[:outs] + r[outs:]


def part(ref, i, n):
    return ref[pl.ds(i * n, n), :]


def put_across(ref, i, v):
    ref[pl.ds(i, T, stride=T), :] = v


def arrive_xy_kernel(tiles_ref, out_ref):
    for lo in range(8):
        v = tiles_ref[pl.ds(lo, NZ, stride=8), :].T
        for hi in range(4):
            put_across(out_ref, 8 * hi + lo, v[T * hi : T * (hi + 1)])


def arrive_yx_kernel(tiles_ref, out_ref):
    for lo in range(8):
        v = tiles_ref[pl.ds(lo, NZ, stride=8), :].T
        for hi in range(4):
            out_ref[pl.ds(T * (8 * hi + lo), T), :] = v[T * hi : T * (hi + 1)]


def blur_kernel(my_ref, mz_ref, up, cur, down, out_ref):
    my, mz = my_ref[...], mz_ref[...]
    for x in range(0, T, 4):
        rows = []
        for i in (x, x + 2):
            columns = [
                jnp.concatenate([part(up, k, HALF), part(cur, k, T), part(down, k, HALF)], axis=0)
                for k in (i, i + 1)
            ]
            r = y_pass(columns, my)
            rows += [r[:, :NZ], r[:, NZ:]]
        w = z_pass(jnp.concatenate(rows, axis=0), mz)
        for i in range(4):
            put_across(out_ref, x + i, w[T * i : T * (i + 1)])


def quotient_kernel(m_ref, own_ref, nbr_ref, obs_ref, q_ref):
    m = m_ref[...]
    for y in range(0, T, 2):
        pair = (y, y + 1)
        blurred = x_pass([part(own_ref, k, T) for k in pair], [part(nbr_ref, k, T) for k in pair], m)
        for k, b in zip(pair, blurred):
            q_ref[pl.ds(k * T, T), :] = part(obs_ref, k, T) / b


def back_kernel(mx_ref, mz_ref, own_ref, nbr_ref, out_ref):
    mx, mz = mx_ref[...], mz_ref[...]
    for y in range(0, T, 4):
        rows = []
        for i in (y, y + 2):
            pair = (i, i + 1)
            rows += x_pass([part(own_ref, k, T) for k in pair], [part(nbr_ref, k, T) for k in pair], mx)
        w = z_pass(jnp.concatenate(rows, axis=0), mz)
        for i in range(4):
            put_across(out_ref, y + i, w[T * i : T * (i + 1)])


def update_kernel(
    back_ref, fwd_ref, mz_ref, up, own, down, cur_up, cur, cur_down, new_ref, out_ref
):
    back, fwd, mz = back_ref[...], fwd_ref[...], mz_ref[...]
    for x in range(0, T, 4):
        rows = []
        for i in (x, x + 2):
            pair = (i, i + 1)
            r = y_pass([jnp.concatenate([part(p, k, T) for p in (up, own, down)], axis=0) for k in pair], back)
            wide = []
            for n, k in enumerate(pair):
                old = jnp.concatenate(
                    [part(cur_up, k, HALF), part(cur, k, T), part(cur_down, k, HALF)], axis=0
                )
                new = old * r[:, NZ * n : NZ * (n + 1)]
                new_ref[pl.ds(k * T, T), :] = new[HALF : HALF + T]
                wide.append(new)
            r = y_pass(wide, fwd)
            rows += [r[:, :NZ], r[:, NZ:]]
        w = z_pass(jnp.concatenate(rows, axis=0), mz)
        for i in range(4):
            put_across(out_ref, x + i, w[T * i : T * (i + 1)])


def leave_kernel(m_ref, up, own, down, cur_ref, tiles_ref, work):
    m = m_ref[...]
    for x in range(0, T, 2):
        pair = (x, x + 1)
        columns = [
            jnp.concatenate([part(up, k, HALF), part(own, k, T), part(down, k, HALF)], axis=0)
            for k in pair
        ]
        r = y_pass(columns, m)
        for n, k in enumerate(pair):
            work[pl.ds(k * T, T), :] = part(cur_ref, k, T) * r[:, NZ * n : NZ * (n + 1)]
    for lo in range(8):
        v = [work[pl.ds(8 * hi + lo, T, stride=T), :] for hi in range(4)]
        tiles_ref[pl.ds(lo, NZ, stride=8), :] = jnp.concatenate(v, axis=0).T


def local(observed, estimate, psf_lateral, psf_axial):
    n_z, n_y = lax.axis_size("gz"), lax.axis_size("gy")
    gz, gy = lax.axis_index("gz").astype(jnp.int32), lax.axis_index("gy").astype(jnp.int32)
    odd = gy % 2 == 1
    side = 1 - 2 * (gy % 2)
    joint = ("gz", "gy")

    def turn(sign):
        pairs = []
        for z in range(n_z):
            for y in range(n_y):
                s = sign * (1 if y % 2 == 0 else -1)
                pairs.append(((z + s) % n_z * n_y + y, z * n_y + y))
        return pairs

    ahead, behind = turn(1), turn(-1)
    outer = [p for i in range(1, n_y - 1, 2) for p in ((i, i + 1), (i + 1, i))]
    inner = [p for i in range(0, n_y, 2) for p in ((i, i + 1), (i + 1, i))]

    def y_swap(to_outer, to_inner):
        from_outer = lax.ppermute(to_outer, "gy", outer)
        from_inner = lax.ppermute(to_inner, "gy", inner)
        return jnp.where(odd, from_inner, from_outer), jnp.where(odd, from_outer, from_inner)

    def y_halves(v):
        v = v.reshape(T, T, NZ)
        first, second = v[:, :HALF], v[:, HALF:]
        swapped = y_swap(jnp.where(odd, second, first), jnp.where(odd, first, second))
        return [h.reshape(T * HALF, NZ) for h in swapped]

    def exchange(tiles):
        return lax.all_to_all(tiles, "gz", split_axis=0, concat_axis=0, tiled=True)

    tiles_shape = (TILES, 4, 8, 128)
    flat = (NZ * 8, 128)
    block_shape = (4, T, NX)
    dma = lambda n: pltpu.SemaphoreType.DMA((n,))
    est_tiles = pl.pallas_call(
        depart_kernel,
        out_shape=jax.ShapeDtypeStruct(tiles_shape, F32),
        in_specs=[pl.BlockSpec(memory_space=pl.ANY)],
        out_specs=pl.BlockSpec(memory_space=pl.ANY),
        scratch_shapes=[pltpu.VMEM(block_shape, F32), pltpu.VMEM(tiles_shape, F32), dma(4), dma(4)],
        cost_estimate=pl.CostEstimate(flops=1_000_000, bytes_accessed=2_000_000, transcendentals=0),
        compiler_params=pltpu.CompilerParams(vmem_limit_bytes=60 * 1024 * 1024),
    )(estimate)
    place = jnp.stack([gz, side, jnp.where(odd, H, NX - H).astype(jnp.int32)])
    obs_tiles, z_fwd, z_bwd, x_fwd, x_bwd, y_fwd, y_bwd, y_wide = call(
        prepare_kernel,
        [(tiles_shape, F32)]
        + [((2 * NZ, 2 * NZ), BF16)] * 2
        + [((2 * T, 4 * T), BF16)] * 2
        + [((2 * T, 4 * T), BF16)] * 2
        + [((4 * T, 6 * T), BF16)],
        [place, psf_lateral, jnp.pad(psf_axial, (0, 2 * NZ - 2 * G - 1)).reshape(1, 2 * NZ), observed],
        smem=(0, 1),
        scratch=[pltpu.VMEM((4, T, NX), F32)],
    )
    est_tiles = exchange(est_tiles)
    obs_tiles = exchange(obs_tiles)
    whole = [(flat, F32)]
    (current,) = call(arrive_xy_kernel, whole, [est_tiles.reshape(flat)])
    (obs,) = call(arrive_yx_kernel, whole, [obs_tiles.reshape(flat)])
    above, below = y_halves(current)
    (own,) = call(blur_kernel, whole, [y_fwd, z_fwd, above, current, below])
    for step in range(ITERS):
        (own,) = call(quotient_kernel, whole, [x_fwd, own, lax.ppermute(own, joint, ahead), obs])
        (own,) = call(back_kernel, whole, [x_bwd, z_bwd, own, lax.ppermute(own, joint, behind)])
        if step < ITERS - 1:
            up, down = y_swap(own, own)
            current, own = call(
                update_kernel,
                whole * 2,
                [y_wide, y_fwd, z_fwd, up, own, down, above, current, below],
            )
        else:
            up, down = y_halves(own)
            (tiles,) = call(
                leave_kernel, whole, [y_bwd, up, own, down, current], scratch=[pltpu.VMEM(flat, F32)]
            )
    tiles = exchange(tiles.reshape(tiles_shape))
    tile_block = ((TILES, 1, 8, 128), 1)
    row_block = ((1, T, NX), 0)
    return per_plane(from_tiles_kernel, block_shape, tile_block, row_block, tiles)


def solution(mesh):
    in_specs = (P("gz", "gy", None), P("gz", "gy", None), P(), P())
    out_specs = P("gz", "gy", None)
    return jax.shard_map(local, mesh=mesh, in_specs=in_specs, out_specs=out_specs, check_vma=False)
```

```python
import functools
import jax
import jax.numpy as jnp
from jax import lax
from jax.experimental import pallas as pl
from jax.experimental.pallas import tpu as pltpu
from jax.sharding import PartitionSpec as P

ITERS = 2
F32 = jnp.float32
BF16 = jnp.bfloat16
H = 15
TAPS = 2 * H + 1
G = 64
T = 32
HALF = T // 2
NX = 1024
TILES = NX // T
NZ = 128
ORDER = [h * 16 + z for k in range(8) for z in (k, 15 - k) for h in range(2)]
PLACE = [ORDER.index(t) for t in range(TILES)]

VMEM = pl.BlockSpec(memory_space=pltpu.VMEM)
SMEM = pl.BlockSpec(memory_space=pltpu.SMEM)


def call(body, outs, operands, smem=(), flops=4_000_000, moved=2_000_000, scratch=()):
    return pl.pallas_call(
        body,
        out_shape=[jax.ShapeDtypeStruct(s, d) for s, d in outs],
        in_specs=[SMEM if i in smem else VMEM for i in range(len(operands))],
        out_specs=[VMEM] * len(outs),
        scratch_shapes=list(scratch),
        cost_estimate=pl.CostEstimate(flops=flops, bytes_accessed=moved, transcendentals=0),
        compiler_params=pltpu.CompilerParams(vmem_limit_bytes=24 * 1024 * 1024),
    )(*operands)


def split(v):
    hi = v.astype(BF16)
    return hi, (v - hi.astype(F32)).astype(BF16)


def swap_groups(rows):
    lane = lax.broadcasted_iota(jnp.int32, rows[0].shape, 1)
    low64, low32 = lane < 64, (lane & 32) == 0
    a, b, c, d = rows
    a, c = jnp.where(low64, a, pltpu.roll(c, 64, 1)), jnp.where(low64, pltpu.roll(a, 64, 1), c)
    b, d = jnp.where(low64, b, pltpu.roll(d, 64, 1)), jnp.where(low64, pltpu.roll(b, 64, 1), d)
    a, b = jnp.where(low32, a, pltpu.roll(b, 32, 1)), jnp.where(low32, pltpu.roll(a, 96, 1), b)
    c, d = jnp.where(low32, c, pltpu.roll(d, 32, 1)), jnp.where(low32, pltpu.roll(c, 96, 1), d)
    return a, b, c, d


def tiles_of(read, write):
    for th in range(8):
        rows = [read(pl.ds(8 * yh, 8), pl.ds(128 * th, 128)) for yh in range(4)]
        for tl, tile in enumerate(swap_groups(rows)):
            write(4 * th + tl, tile)


def depart_kernel(block_hbm, tiles_hbm, block, tiles, in_sems, out_sems):
    copies = [pltpu.make_async_copy(block_hbm.at[z], block.at[z], in_sems.at[z]) for z in range(4)]
    for c in copies:
        c.start()
    for z in range(4):
        copies[z].wait()
        for th in range(8):
            rows = [block[z, pl.ds(8 * yh, 8), pl.ds(128 * th, 128)] for yh in range(4)]
            for tl, tile in enumerate(swap_groups(rows)):
                tiles[PLACE[4 * th + tl], z] = tile
    sent = []
    for i in range(4):
        group = pl.ds(8 * i, 8)
        sent.append(pltpu.make_async_copy(tiles.at[group], tiles_hbm.at[group], out_sems.at[i]))
        sent[-1].start()
    for c in sent:
        c.wait()


def from_tiles_kernel(tiles_ref, out_ref):
    for th in range(8):
        tiles = [tiles_ref[PLACE[4 * th + tl], 0] for tl in range(4)]
        for yh, row in enumerate(swap_groups(tiles)):
            out_ref[0, pl.ds(8 * yh, 8), pl.ds(128 * th, 128)] = row


def per_plane(body, out_shape, in_block, out_block, operand):
    def spec(block):
        shape, dim = block
        return pl.BlockSpec(shape, lambda z: tuple(z if d == dim else 0 for d in range(len(shape))))

    return pl.pallas_call(
        body,
        grid=(4,),
        out_shape=jax.ShapeDtypeStruct(out_shape, F32),
        in_specs=[spec(in_block)],
        out_specs=spec(out_block),
        cost_estimate=pl.CostEstimate(flops=1_000_000, bytes_accessed=2_000_000, transcendentals=0),
        compiler_params=pltpu.CompilerParams(vmem_limit_bytes=24 * 1024 * 1024),
    )(operand)


def prepare_kernel(
    place_ref, lat_ref, ax_ref, obs_ref, obs_tiles, z_fwd, z_bwd, x_fwd, x_bwd, y_fwd, y_bwd, y_wide, rolled
):
    tile, side = place_ref[0], place_ref[1]
    for z in range(4):
        rolled[z] = pltpu.roll(obs_ref[z], place_ref[2], 1)

        def write(t, v, z=z):
            obs_tiles[PLACE[t], z] = v

        tiles_of(lambda rows, lanes, z=z: rolled[z, rows, lanes], write)
    band = pltpu.roll(ax_ref[...], 2 * NZ - G, 1)
    band = band / jnp.sum(band)
    wide = jnp.broadcast_to(band, (NZ, 2 * NZ))
    back = pltpu.roll(wide, 0, 1, stride=1, stride_axis=0)[:, :NZ]
    for m, ref in ((back.T, z_fwd), (back, z_bwd)):
        hi, lo = split(m)
        ref[pl.ds(0, NZ), pl.ds(0, NZ)] = hi
        ref[pl.ds(NZ, NZ), pl.ds(0, NZ)] = hi
        ref[pl.ds(0, NZ), pl.ds(NZ, NZ)] = lo
        ref[pl.ds(NZ, NZ), pl.ds(NZ, NZ)] = jnp.zeros_like(lo)
    total = lat_ref[0]
    for k in range(1, TAPS):
        total = total + lat_ref[k]
    for flip, outs, ins, ref in ((0, T, 2 * T, y_fwd), (1, T, 2 * T, y_bwd), (1, 2 * T, 3 * T, y_wide)):
        row = lax.broadcasted_iota(jnp.int32, (outs, 2 * NZ), 0)
        lane = lax.broadcasted_iota(jnp.int32, (outs, 2 * NZ), 1)
        high = lane < ins
        d = jnp.where(high, lane, lane - ins) - row - 1
        m = jnp.zeros((outs, 2 * NZ), F32)
        for k in range(TAPS):
            m = jnp.where(d == k, lat_ref[TAPS - 1 - k if flip else k], m)
        hi, lo = split(m)
        ref[pl.ds(0, outs), :] = hi[:, : 2 * ins]
        ref[pl.ds(outs, outs), :] = jnp.where(high, lo.astype(F32), 0.0).astype(BF16)[:, : 2 * ins]
    row = lax.broadcasted_iota(jnp.int32, (T, NZ), 0)
    lane = lax.broadcasted_iota(jnp.int32, (T, NZ), 1)
    own, first = lane < 64, (lane & 32) == 0
    col = lane & 31
    here = T * tile
    shifted = here + H * side
    wrap = lambda v: v & (NX - 1)
    src_f = wrap(jnp.where(own, here, here + T * side) + col)
    dst_f = wrap(shifted + row)
    src_b = wrap(jnp.where(own, shifted, shifted - T * side) + col)
    dst_b = wrap(here + row)
    for d, ref in ((src_f - dst_f, x_fwd), (dst_b - src_b, x_bwd)):
        m = jnp.zeros((T, NZ), F32)
        for k in range(TAPS):
            m = jnp.where(d == k - H, lat_ref[k], m)
        scale = jnp.full((T, NZ), total, F32)
        m = m / scale / scale
        hi, lo = split(m)
        ref[pl.ds(0, T), :] = hi
        ref[pl.ds(T, T), :] = jnp.where(first, lo.astype(F32), 0.0).astype(BF16)


def z_pass(v, m):
    r = jnp.dot(jnp.concatenate(split(v), axis=1), m, preferred_element_type=F32)
    return r[:, :NZ] + r[:, NZ:]


def x_pass(own, nbr, m):
    columns = []
    for o, n in zip(own, nbr):
        columns.append(jnp.concatenate([*split(o), *split(n)], axis=0))
    r = jnp.dot(m, jnp.concatenate(columns, axis=1), preferred_element_type=F32)
    r = r[:T] + r[T:]
    return [r[:, NZ * i : NZ * (i + 1)] for i in range(len(own))]


def y_pass(columns, m):
    outs = m.shape[0] // 2
    stacked = [jnp.concatenate(split(c), axis=0) for c in columns]
    r = jnp.dot(m, jnp.concatenate(stacked, axis=1), preferred_element_type=F32)
    return r[:outs] + r[outs:]


def part(ref, i, n):
    return ref[pl.ds(i * n, n), :]


def put_across(ref, i, v):
    ref[pl.ds(i, T, stride=T), :] = v


def in_order(tiles_ref, planes):
    for s in range(TILES):
        planes[pl.ds(32 * s, 32), :] = part(tiles_ref, PLACE[s], 32)


def arrive_xy_kernel(tiles_ref, out_ref, planes):
    in_order(tiles_ref, planes)
    for lo in range(8):
        v = planes[pl.ds(lo, NZ, stride=8), :].T
        for hi in range(4):
            put_across(out_ref, 8 * hi + lo, v[T * hi : T * (hi + 1)])


def arrive_yx_kernel(tiles_ref, out_ref, planes):
    in_order(tiles_ref, planes)
    for lo in range(8):
        v = planes[pl.ds(lo, NZ, stride=8), :].T
        for hi in range(4):
            out_ref[pl.ds(T * (8 * hi + lo), T), :] = v[T * hi : T * (hi + 1)]


def blur_kernel(my_ref, mz_ref, up, cur, down, out_ref):
    my, mz = my_ref[...], mz_ref[...]
    for x in range(0, T, 4):
        rows = []
        for i in (x, x + 2):
            columns = [
                jnp.concatenate([part(up, k, HALF), part(cur, k, T), part(down, k, HALF)], axis=0)
                for k in (i, i + 1)
            ]
            r = y_pass(columns, my)
            rows += [r[:, :NZ], r[:, NZ:]]
        w = z_pass(jnp.concatenate(rows, axis=0), mz)
        for i in range(4):
            put_across(out_ref, x + i, w[T * i : T * (i + 1)])


def quotient_kernel(m_ref, own_ref, nbr_ref, obs_ref, q_ref):
    m = m_ref[...]
    for y in range(0, T, 2):
        pair = (y, y + 1)
        blurred = x_pass([part(own_ref, k, T) for k in pair], [part(nbr_ref, k, T) for k in pair], m)
        for k, b in zip(pair, blurred):
            q_ref[pl.ds(k * T, T), :] = part(obs_ref, k, T) / b


def back_kernel(mx_ref, mz_ref, own_ref, nbr_ref, out_ref):
    mx, mz = mx_ref[...], mz_ref[...]
    for y in range(0, T, 4):
        rows = []
        for i in (y, y + 2):
            pair = (i, i + 1)
            rows += x_pass([part(own_ref, k, T) for k in pair], [part(nbr_ref, k, T) for k in pair], mx)
        w = z_pass(jnp.concatenate(rows, axis=0), mz)
        for i in range(4):
            put_across(out_ref, y + i, w[T * i : T * (i + 1)])


def update_kernel(
    back_ref, fwd_ref, mz_ref, up, own, down, cur_up, cur, cur_down, new_ref, out_ref
):
    back, fwd, mz = back_ref[...], fwd_ref[...], mz_ref[...]
    for x in range(0, T, 4):
        rows = []
        for i in (x, x + 2):
            pair = (i, i + 1)
            r = y_pass([jnp.concatenate([part(p, k, T) for p in (up, own, down)], axis=0) for k in pair], back)
            wide = []
            for n, k in enumerate(pair):
                old = jnp.concatenate(
                    [part(cur_up, k, HALF), part(cur, k, T), part(cur_down, k, HALF)], axis=0
                )
                new = old * r[:, NZ * n : NZ * (n + 1)]
                new_ref[pl.ds(k * T, T), :] = new[HALF : HALF + T]
                wide.append(new)
            r = y_pass(wide, fwd)
            rows += [r[:, :NZ], r[:, NZ:]]
        w = z_pass(jnp.concatenate(rows, axis=0), mz)
        for i in range(4):
            put_across(out_ref, x + i, w[T * i : T * (i + 1)])


def leave_kernel(m_ref, up, own, down, cur_ref, tiles_ref, work, planes):
    m = m_ref[...]
    for x in range(0, T, 2):
        pair = (x, x + 1)
        columns = [
            jnp.concatenate([part(up, k, HALF), part(own, k, T), part(down, k, HALF)], axis=0)
            for k in pair
        ]
        r = y_pass(columns, m)
        for n, k in enumerate(pair):
            work[pl.ds(k * T, T), :] = part(cur_ref, k, T) * r[:, NZ * n : NZ * (n + 1)]
    for lo in range(8):
        v = [work[pl.ds(8 * hi + lo, T, stride=T), :] for hi in range(4)]
        planes[pl.ds(lo, NZ, stride=8), :] = jnp.concatenate(v, axis=0).T
    for s in range(TILES):
        tiles_ref[pl.ds(32 * PLACE[s], 32), :] = part(planes, s, 32)


def local(observed, estimate, psf_lateral, psf_axial):
    n_z, n_y = lax.axis_size("gz"), lax.axis_size("gy")
    gz, gy = lax.axis_index("gz").astype(jnp.int32), lax.axis_index("gy").astype(jnp.int32)
    odd = gy % 2 == 1
    side = 1 - 2 * (gy % 2)
    joint = ("gz", "gy")

    def turn(sign):
        pairs = []
        for z in range(n_z):
            for y in range(n_y):
                s = sign * (1 if y % 2 == 0 else -1)
                pairs.append(((z + s) % n_z * n_y + y, z * n_y + y))
        return pairs

    ahead, behind = turn(1), turn(-1)
    outer = [p for i in range(1, n_y - 1, 2) for p in ((i, i + 1), (i + 1, i))]
    inner = [p for i in range(0, n_y, 2) for p in ((i, i + 1), (i + 1, i))]

    def y_swap(to_outer, to_inner):
        from_outer = lax.ppermute(to_outer, "gy", outer)
        from_inner = lax.ppermute(to_inner, "gy", inner)
        return jnp.where(odd, from_inner, from_outer), jnp.where(odd, from_outer, from_inner)

    def y_halves(v):
        v = v.reshape(T, T, NZ)
        first, second = v[:, :HALF], v[:, HALF:]
        swapped = y_swap(jnp.where(odd, second, first), jnp.where(odd, first, second))
        return [h.reshape(T * HALF, NZ) for h in swapped]

    def exchange(tiles):
        return lax.all_to_all(
            tiles, "gz", split_axis=0, concat_axis=0, tiled=True, axis_index_groups=[ORDER]
        )

    tiles_shape = (TILES, 4, 8, 128)
    flat = (NZ * 8, 128)
    block_shape = (4, T, NX)
    dma = lambda n: pltpu.SemaphoreType.DMA((n,))
    est_tiles = pl.pallas_call(
        depart_kernel,
        out_shape=jax.ShapeDtypeStruct(tiles_shape, F32),
        in_specs=[pl.BlockSpec(memory_space=pl.ANY)],
        out_specs=pl.BlockSpec(memory_space=pl.ANY),
        scratch_shapes=[pltpu.VMEM(block_shape, F32), pltpu.VMEM(tiles_shape, F32), dma(4), dma(4)],
        cost_estimate=pl.CostEstimate(flops=1_000_000, bytes_accessed=2_000_000, transcendentals=0),
        compiler_params=pltpu.CompilerParams(vmem_limit_bytes=60 * 1024 * 1024),
    )(estimate)
    place = jnp.stack([gz, side, jnp.where(odd, H, NX - H).astype(jnp.int32)])
    obs_tiles, z_fwd, z_bwd, x_fwd, x_bwd, y_fwd, y_bwd, y_wide = call(
        prepare_kernel,
        [(tiles_shape, F32)]
        + [((2 * NZ, 2 * NZ), BF16)] * 2
        + [((2 * T, 4 * T), BF16)] * 2
        + [((2 * T, 4 * T), BF16)] * 2
        + [((4 * T, 6 * T), BF16)],
        [place, psf_lateral, jnp.pad(psf_axial, (0, 2 * NZ - 2 * G - 1)).reshape(1, 2 * NZ), observed],
        smem=(0, 1),
        scratch=[pltpu.VMEM((4, T, NX), F32)],
    )
    est_tiles = exchange(est_tiles)
    obs_tiles = exchange(obs_tiles)
    whole = [(flat, F32)]
    planes = [pltpu.VMEM(flat, F32)]
    (current,) = call(arrive_xy_kernel, whole, [est_tiles.reshape(flat)], scratch=planes)
    (obs,) = call(arrive_yx_kernel, whole, [obs_tiles.reshape(flat)], scratch=planes)
    above, below = y_halves(current)
    (own,) = call(blur_kernel, whole, [y_fwd, z_fwd, above, current, below])
    for step in range(ITERS):
        (own,) = call(quotient_kernel, whole, [x_fwd, own, lax.ppermute(own, joint, ahead), obs])
        (own,) = call(back_kernel, whole, [x_bwd, z_bwd, own, lax.ppermute(own, joint, behind)])
        if step < ITERS - 1:
            up, down = y_swap(own, own)
            current, own = call(
                update_kernel,
                whole * 2,
                [y_wide, y_fwd, z_fwd, up, own, down, above, current, below],
            )
        else:
            up, down = y_halves(own)
            (tiles,) = call(
                leave_kernel, whole, [y_bwd, up, own, down, current], scratch=planes * 2
            )
    tiles = exchange(tiles.reshape(tiles_shape))
    tile_block = ((TILES, 1, 8, 128), 1)
    row_block = ((1, T, NX), 0)
    return per_plane(from_tiles_kernel, block_shape, tile_block, row_block, tiles)


def solution(mesh):
    in_specs = (P("gz", "gy", None), P("gz", "gy", None), P(), P())
    out_specs = P("gz", "gy", None)
    return jax.shard_map(local, mesh=mesh, in_specs=in_specs, out_specs=out_specs, check_vma=False)
```

```python
import functools
import jax
import jax.numpy as jnp
from jax import lax
from jax.experimental import pallas as pl
from jax.experimental.pallas import tpu as pltpu
from jax.sharding import PartitionSpec as P

ITERS = 2
F32 = jnp.float32
BF16 = jnp.bfloat16
H = 15
TAPS = 2 * H + 1
G = 64
T = 32
HALF = T // 2
NX = 1024
TILES = NX // T
NZ = 128
ORDER = [h * 16 + int(format(i, '04b')[::-1], 2) for i in range(16) for h in range(2)]
PLACE = [ORDER.index(t) for t in range(TILES)]

VMEM = pl.BlockSpec(memory_space=pltpu.VMEM)
SMEM = pl.BlockSpec(memory_space=pltpu.SMEM)


def call(body, outs, operands, smem=(), flops=4_000_000, moved=2_000_000, scratch=()):
    return pl.pallas_call(
        body,
        out_shape=[jax.ShapeDtypeStruct(s, d) for s, d in outs],
        in_specs=[SMEM if i in smem else VMEM for i in range(len(operands))],
        out_specs=[VMEM] * len(outs),
        scratch_shapes=list(scratch),
        cost_estimate=pl.CostEstimate(flops=flops, bytes_accessed=moved, transcendentals=0),
        compiler_params=pltpu.CompilerParams(vmem_limit_bytes=24 * 1024 * 1024),
    )(*operands)


def split(v):
    hi = v.astype(BF16)
    return hi, (v - hi.astype(F32)).astype(BF16)


def swap_groups(rows):
    lane = lax.broadcasted_iota(jnp.int32, rows[0].shape, 1)
    low64, low32 = lane < 64, (lane & 32) == 0
    a, b, c, d = rows
    a, c = jnp.where(low64, a, pltpu.roll(c, 64, 1)), jnp.where(low64, pltpu.roll(a, 64, 1), c)
    b, d = jnp.where(low64, b, pltpu.roll(d, 64, 1)), jnp.where(low64, pltpu.roll(b, 64, 1), d)
    a, b = jnp.where(low32, a, pltpu.roll(b, 32, 1)), jnp.where(low32, pltpu.roll(a, 96, 1), b)
    c, d = jnp.where(low32, c, pltpu.roll(d, 32, 1)), jnp.where(low32, pltpu.roll(c, 96, 1), d)
    return a, b, c, d


def tiles_of(read, write):
    for th in range(8):
        rows = [read(pl.ds(8 * yh, 8), pl.ds(128 * th, 128)) for yh in range(4)]
        for tl, tile in enumerate(swap_groups(rows)):
            write(4 * th + tl, tile)


def depart_kernel(block_hbm, tiles_hbm, block, tiles, in_sems, out_sems):
    copies = [pltpu.make_async_copy(block_hbm.at[z], block.at[z], in_sems.at[z]) for z in range(4)]
    for c in copies:
        c.start()
    for z in range(4):
        copies[z].wait()
        for th in range(8):
            rows = [block[z, pl.ds(8 * yh, 8), pl.ds(128 * th, 128)] for yh in range(4)]
            for tl, tile in enumerate(swap_groups(rows)):
                tiles[PLACE[4 * th + tl], z] = tile
    sent = []
    for i in range(4):
        group = pl.ds(8 * i, 8)
        sent.append(pltpu.make_async_copy(tiles.at[group], tiles_hbm.at[group], out_sems.at[i]))
        sent[-1].start()
    for c in sent:
        c.wait()


def from_tiles_kernel(tiles_ref, out_ref):
    for th in range(8):
        tiles = [tiles_ref[PLACE[4 * th + tl], 0] for tl in range(4)]
        for yh, row in enumerate(swap_groups(tiles)):
            out_ref[0, pl.ds(8 * yh, 8), pl.ds(128 * th, 128)] = row


def per_plane(body, out_shape, in_block, out_block, operand):
    def spec(block):
        shape, dim = block
        return pl.BlockSpec(shape, lambda z: tuple(z if d == dim else 0 for d in range(len(shape))))

    return pl.pallas_call(
        body,
        grid=(4,),
        out_shape=jax.ShapeDtypeStruct(out_shape, F32),
        in_specs=[spec(in_block)],
        out_specs=spec(out_block),
        cost_estimate=pl.CostEstimate(flops=1_000_000, bytes_accessed=2_000_000, transcendentals=0),
        compiler_params=pltpu.CompilerParams(vmem_limit_bytes=24 * 1024 * 1024),
    )(operand)


def prepare_kernel(
    place_ref, lat_ref, ax_ref, obs_ref, obs_tiles, z_fwd, z_bwd, x_fwd, x_bwd, y_fwd, y_bwd, y_wide, rolled
):
    tile, side = place_ref[0], place_ref[1]
    for z in range(4):
        rolled[z] = pltpu.roll(obs_ref[z], place_ref[2], 1)

        def write(t, v, z=z):
            obs_tiles[PLACE[t], z] = v

        tiles_of(lambda rows, lanes, z=z: rolled[z, rows, lanes], write)
    band = pltpu.roll(ax_ref[...], 2 * NZ - G, 1)
    band = band / jnp.sum(band)
    wide = jnp.broadcast_to(band, (NZ, 2 * NZ))
    back = pltpu.roll(wide, 0, 1, stride=1, stride_axis=0)[:, :NZ]
    for m, ref in ((back.T, z_fwd), (back, z_bwd)):
        hi, lo = split(m)
        ref[pl.ds(0, NZ), pl.ds(0, NZ)] = hi
        ref[pl.ds(NZ, NZ), pl.ds(0, NZ)] = hi
        ref[pl.ds(0, NZ), pl.ds(NZ, NZ)] = lo
        ref[pl.ds(NZ, NZ), pl.ds(NZ, NZ)] = jnp.zeros_like(lo)
    total = lat_ref[0]
    for k in range(1, TAPS):
        total = total + lat_ref[k]
    for flip, outs, ins, ref in ((0, T, 2 * T, y_fwd), (1, T, 2 * T, y_bwd), (1, 2 * T, 3 * T, y_wide)):
        row = lax.broadcasted_iota(jnp.int32, (outs, 2 * NZ), 0)
        lane = lax.broadcasted_iota(jnp.int32, (outs, 2 * NZ), 1)
        high = lane < ins
        d = jnp.where(high, lane, lane - ins) - row - 1
        m = jnp.zeros((outs, 2 * NZ), F32)
        for k in range(TAPS):
            m = jnp.where(d == k, lat_ref[TAPS - 1 - k if flip else k], m)
        hi, lo = split(m)
        ref[pl.ds(0, outs), :] = hi[:, : 2 * ins]
        ref[pl.ds(outs, outs), :] = jnp.where(high, lo.astype(F32), 0.0).astype(BF16)[:, : 2 * ins]
    row = lax.broadcasted_iota(jnp.int32, (T, NZ), 0)
    lane = lax.broadcasted_iota(jnp.int32, (T, NZ), 1)
    own, first = lane < 64, (lane & 32) == 0
    col = lane & 31
    here = T * tile
    shifted = here + H * side
    wrap = lambda v: v & (NX - 1)
    src_f = wrap(jnp.where(own, here, here + T * side) + col)
    dst_f = wrap(shifted + row)
    src_b = wrap(jnp.where(own, shifted, shifted - T * side) + col)
    dst_b = wrap(here + row)
    for d, ref in ((src_f - dst_f, x_fwd), (dst_b - src_b, x_bwd)):
        m = jnp.zeros((T, NZ), F32)
        for k in range(TAPS):
            m = jnp.where(d == k - H, lat_ref[k], m)
        scale = jnp.full((T, NZ), total, F32)
        m = m / scale / scale
        hi, lo = split(m)
        ref[pl.ds(0, T), :] = hi
        ref[pl.ds(T, T), :] = jnp.where(first, lo.astype(F32), 0.0).astype(BF16)


def z_pass(v, m):
    r = jnp.dot(jnp.concatenate(split(v), axis=1), m, preferred_element_type=F32)
    return r[:, :NZ] + r[:, NZ:]


def x_pass(own, nbr, m):
    columns = []
    for o, n in zip(own, nbr):
        columns.append(jnp.concatenate([*split(o), *split(n)], axis=0))
    r = jnp.dot(m, jnp.concatenate(columns, axis=1), preferred_element_type=F32)
    r = r[:T] + r[T:]
    return [r[:, NZ * i : NZ * (i + 1)] for i in range(len(own))]


def y_pass(columns, m):
    outs = m.shape[0] // 2
    stacked = [jnp.concatenate(split(c), axis=0) for c in columns]
    r = jnp.dot(m, jnp.concatenate(stacked, axis=1), preferred_element_type=F32)
    return r[:outs] + r[outs:]


def part(ref, i, n):
    return ref[pl.ds(i * n, n), :]


def put_across(ref, i, v):
    ref[pl.ds(i, T, stride=T), :] = v


def in_order(tiles_ref, planes):
    for s in range(TILES):
        planes[pl.ds(32 * s, 32), :] = part(tiles_ref, PLACE[s], 32)


def arrive_xy_kernel(tiles_ref, out_ref, planes):
    in_order(tiles_ref, planes)
    for lo in range(8):
        v = planes[pl.ds(lo, NZ, stride=8), :].T
        for hi in range(4):
            put_across(out_ref, 8 * hi + lo, v[T * hi : T * (hi + 1)])


def arrive_yx_kernel(tiles_ref, out_ref, planes):
    in_order(tiles_ref, planes)
    for lo in range(8):
        v = planes[pl.ds(lo, NZ, stride=8), :].T
        for hi in range(4):
            out_ref[pl.ds(T * (8 * hi + lo), T), :] = v[T * hi : T * (hi + 1)]


def blur_kernel(my_ref, mz_ref, up, cur, down, out_ref):
    my, mz = my_ref[...], mz_ref[...]
    for x in range(0, T, 4):
        rows = []
        for i in (x, x + 2):
            columns = [
                jnp.concatenate([part(up, k, HALF), part(cur, k, T), part(down, k, HALF)], axis=0)
                for k in (i, i + 1)
            ]
            r = y_pass(columns, my)
            rows += [r[:, :NZ], r[:, NZ:]]
        w = z_pass(jnp.concatenate(rows, axis=0), mz)
        for i in range(4):
            put_across(out_ref, x + i, w[T * i : T * (i + 1)])


def quotient_kernel(m_ref, own_ref, nbr_ref, obs_ref, q_ref):
    m = m_ref[...]
    for y in range(0, T, 2):
        pair = (y, y + 1)
        blurred = x_pass([part(own_ref, k, T) for k in pair], [part(nbr_ref, k, T) for k in pair], m)
        for k, b in zip(pair, blurred):
            q_ref[pl.ds(k * T, T), :] = part(obs_ref, k, T) / b


def back_kernel(mx_ref, mz_ref, own_ref, nbr_ref, out_ref):
    mx, mz = mx_ref[...], mz_ref[...]
    for y in range(0, T, 4):
        rows = []
        for i in (y, y + 2):
            pair = (i, i + 1)
            rows += x_pass([part(own_ref, k, T) for k in pair], [part(nbr_ref, k, T) for k in pair], mx)
        w = z_pass(jnp.concatenate(rows, axis=0), mz)
        for i in range(4):
            put_across(out_ref, y + i, w[T * i : T * (i + 1)])


def update_kernel(
    back_ref, fwd_ref, mz_ref, up, own, down, cur_up, cur, cur_down, new_ref, out_ref
):
    back, fwd, mz = back_ref[...], fwd_ref[...], mz_ref[...]
    for x in range(0, T, 4):
        rows = []
        for i in (x, x + 2):
            pair = (i, i + 1)
            r = y_pass([jnp.concatenate([part(p, k, T) for p in (up, own, down)], axis=0) for k in pair], back)
            wide = []
            for n, k in enumerate(pair):
                old = jnp.concatenate(
                    [part(cur_up, k, HALF), part(cur, k, T), part(cur_down, k, HALF)], axis=0
                )
                new = old * r[:, NZ * n : NZ * (n + 1)]
                new_ref[pl.ds(k * T, T), :] = new[HALF : HALF + T]
                wide.append(new)
            r = y_pass(wide, fwd)
            rows += [r[:, :NZ], r[:, NZ:]]
        w = z_pass(jnp.concatenate(rows, axis=0), mz)
        for i in range(4):
            put_across(out_ref, x + i, w[T * i : T * (i + 1)])


def leave_kernel(m_ref, up, own, down, cur_ref, tiles_ref, work, planes):
    m = m_ref[...]
    for x in range(0, T, 2):
        pair = (x, x + 1)
        columns = [
            jnp.concatenate([part(up, k, HALF), part(own, k, T), part(down, k, HALF)], axis=0)
            for k in pair
        ]
        r = y_pass(columns, m)
        for n, k in enumerate(pair):
            work[pl.ds(k * T, T), :] = part(cur_ref, k, T) * r[:, NZ * n : NZ * (n + 1)]
    for lo in range(8):
        v = [work[pl.ds(8 * hi + lo, T, stride=T), :] for hi in range(4)]
        planes[pl.ds(lo, NZ, stride=8), :] = jnp.concatenate(v, axis=0).T
    for s in range(TILES):
        tiles_ref[pl.ds(32 * PLACE[s], 32), :] = part(planes, s, 32)


def local(observed, estimate, psf_lateral, psf_axial):
    n_z, n_y = lax.axis_size("gz"), lax.axis_size("gy")
    gz, gy = lax.axis_index("gz").astype(jnp.int32), lax.axis_index("gy").astype(jnp.int32)
    odd = gy % 2 == 1
    side = 1 - 2 * (gy % 2)
    joint = ("gz", "gy")

    def turn(sign):
        pairs = []
        for z in range(n_z):
            for y in range(n_y):
                s = sign * (1 if y % 2 == 0 else -1)
                pairs.append(((z + s) % n_z * n_y + y, z * n_y + y))
        return pairs

    ahead, behind = turn(1), turn(-1)
    outer = [p for i in range(1, n_y - 1, 2) for p in ((i, i + 1), (i + 1, i))]
    inner = [p for i in range(0, n_y, 2) for p in ((i, i + 1), (i + 1, i))]

    def y_swap(to_outer, to_inner):
        from_outer = lax.ppermute(to_outer, "gy", outer)
        from_inner = lax.ppermute(to_inner, "gy", inner)
        return jnp.where(odd, from_inner, from_outer), jnp.where(odd, from_outer, from_inner)

    def y_halves(v):
        v = v.reshape(T, T, NZ)
        first, second = v[:, :HALF], v[:, HALF:]
        swapped = y_swap(jnp.where(odd, second, first), jnp.where(odd, first, second))
        return [h.reshape(T * HALF, NZ) for h in swapped]

    def exchange(tiles):
        return lax.all_to_all(
            tiles, "gz", split_axis=0, concat_axis=0, tiled=True, axis_index_groups=[ORDER]
        )

    tiles_shape = (TILES, 4, 8, 128)
    flat = (NZ * 8, 128)
    block_shape = (4, T, NX)
    dma = lambda n: pltpu.SemaphoreType.DMA((n,))
    est_tiles = pl.pallas_call(
        depart_kernel,
        out_shape=jax.ShapeDtypeStruct(tiles_shape, F32),
        in_specs=[pl.BlockSpec(memory_space=pl.ANY)],
        out_specs=pl.BlockSpec(memory_space=pl.ANY),
        scratch_shapes=[pltpu.VMEM(block_shape, F32), pltpu.VMEM(tiles_shape, F32), dma(4), dma(4)],
        cost_estimate=pl.CostEstimate(flops=1_000_000, bytes_accessed=2_000_000, transcendentals=0),
        compiler_params=pltpu.CompilerParams(vmem_limit_bytes=60 * 1024 * 1024),
    )(estimate)
    place = jnp.stack([gz, side, jnp.where(odd, H, NX - H).astype(jnp.int32)])
    obs_tiles, z_fwd, z_bwd, x_fwd, x_bwd, y_fwd, y_bwd, y_wide = call(
        prepare_kernel,
        [(tiles_shape, F32)]
        + [((2 * NZ, 2 * NZ), BF16)] * 2
        + [((2 * T, 4 * T), BF16)] * 2
        + [((2 * T, 4 * T), BF16)] * 2
        + [((4 * T, 6 * T), BF16)],
        [place, psf_lateral, jnp.pad(psf_axial, (0, 2 * NZ - 2 * G - 1)).reshape(1, 2 * NZ), observed],
        smem=(0, 1),
        scratch=[pltpu.VMEM((4, T, NX), F32)],
    )
    est_tiles = exchange(est_tiles)
    obs_tiles = exchange(obs_tiles)
    whole = [(flat, F32)]
    planes = [pltpu.VMEM(flat, F32)]
    (current,) = call(arrive_xy_kernel, whole, [est_tiles.reshape(flat)], scratch=planes)
    (obs,) = call(arrive_yx_kernel, whole, [obs_tiles.reshape(flat)], scratch=planes)
    above, below = y_halves(current)
    (own,) = call(blur_kernel, whole, [y_fwd, z_fwd, above, current, below])
    for step in range(ITERS):
        (own,) = call(quotient_kernel, whole, [x_fwd, own, lax.ppermute(own, joint, ahead), obs])
        (own,) = call(back_kernel, whole, [x_bwd, z_bwd, own, lax.ppermute(own, joint, behind)])
        if step < ITERS - 1:
            up, down = y_swap(own, own)
            current, own = call(
                update_kernel,
                whole * 2,
                [y_wide, y_fwd, z_fwd, up, own, down, above, current, below],
            )
        else:
            up, down = y_halves(own)
            (tiles,) = call(
                leave_kernel, whole, [y_bwd, up, own, down, current], scratch=planes * 2
            )
    tiles = exchange(tiles.reshape(tiles_shape))
    tile_block = ((TILES, 1, 8, 128), 1)
    row_block = ((1, T, NX), 0)
    return per_plane(from_tiles_kernel, block_shape, tile_block, row_block, tiles)


def solution(mesh):
    in_specs = (P("gz", "gy", None), P("gz", "gy", None), P(), P())
    out_specs = P("gz", "gy", None)
    return jax.shard_map(local, mesh=mesh, in_specs=in_specs, out_specs=out_specs, check_vma=False)
```

```python
import functools
import jax
import jax.numpy as jnp
from jax import lax
from jax.experimental import pallas as pl
from jax.experimental.pallas import tpu as pltpu
from jax.sharding import PartitionSpec as P

ITERS = 2
F32 = jnp.float32
BF16 = jnp.bfloat16
H = 15
TAPS = 2 * H + 1
G = 64
T = 32
HALF = T // 2
NX = 1024
TILES = NX // T
NZ = 128
ORDER = [h * 16 + int(format(i, '04b')[::-1], 2) for h in range(2) for i in range(16)]
PLACE = [ORDER.index(t) for t in range(TILES)]

VMEM = pl.BlockSpec(memory_space=pltpu.VMEM)
SMEM = pl.BlockSpec(memory_space=pltpu.SMEM)


def call(body, outs, operands, smem=(), flops=4_000_000, moved=2_000_000, scratch=()):
    return pl.pallas_call(
        body,
        out_shape=[jax.ShapeDtypeStruct(s, d) for s, d in outs],
        in_specs=[SMEM if i in smem else VMEM for i in range(len(operands))],
        out_specs=[VMEM] * len(outs),
        scratch_shapes=list(scratch),
        cost_estimate=pl.CostEstimate(flops=flops, bytes_accessed=moved, transcendentals=0),
        compiler_params=pltpu.CompilerParams(vmem_limit_bytes=24 * 1024 * 1024),
    )(*operands)


def split(v):
    hi = v.astype(BF16)
    return hi, (v - hi.astype(F32)).astype(BF16)


def swap_groups(rows):
    lane = lax.broadcasted_iota(jnp.int32, rows[0].shape, 1)
    low64, low32 = lane < 64, (lane & 32) == 0
    a, b, c, d = rows
    a, c = jnp.where(low64, a, pltpu.roll(c, 64, 1)), jnp.where(low64, pltpu.roll(a, 64, 1), c)
    b, d = jnp.where(low64, b, pltpu.roll(d, 64, 1)), jnp.where(low64, pltpu.roll(b, 64, 1), d)
    a, b = jnp.where(low32, a, pltpu.roll(b, 32, 1)), jnp.where(low32, pltpu.roll(a, 96, 1), b)
    c, d = jnp.where(low32, c, pltpu.roll(d, 32, 1)), jnp.where(low32, pltpu.roll(c, 96, 1), d)
    return a, b, c, d


def tiles_of(read, write):
    for th in range(8):
        rows = [read(pl.ds(8 * yh, 8), pl.ds(128 * th, 128)) for yh in range(4)]
        for tl, tile in enumerate(swap_groups(rows)):
            write(4 * th + tl, tile)


def depart_kernel(block_hbm, tiles_hbm, block, tiles, in_sems, out_sems):
    copies = [pltpu.make_async_copy(block_hbm.at[z], block.at[z], in_sems.at[z]) for z in range(4)]
    for c in copies:
        c.start()
    for z in range(4):
        copies[z].wait()
        for th in range(8):
            rows = [block[z, pl.ds(8 * yh, 8), pl.ds(128 * th, 128)] for yh in range(4)]
            for tl, tile in enumerate(swap_groups(rows)):
                tiles[PLACE[4 * th + tl], z] = tile
    sent = []
    for i in range(4):
        group = pl.ds(8 * i, 8)
        sent.append(pltpu.make_async_copy(tiles.at[group], tiles_hbm.at[group], out_sems.at[i]))
        sent[-1].start()
    for c in sent:
        c.wait()


def from_tiles_kernel(tiles_ref, out_ref):
    for th in range(8):
        tiles = [tiles_ref[PLACE[4 * th + tl], 0] for tl in range(4)]
        for yh, row in enumerate(swap_groups(tiles)):
            out_ref[0, pl.ds(8 * yh, 8), pl.ds(128 * th, 128)] = row


def per_plane(body, out_shape, in_block, out_block, operand):
    def spec(block):
        shape, dim = block
        return pl.BlockSpec(shape, lambda z: tuple(z if d == dim else 0 for d in range(len(shape))))

    return pl.pallas_call(
        body,
        grid=(4,),
        out_shape=jax.ShapeDtypeStruct(out_shape, F32),
        in_specs=[spec(in_block)],
        out_specs=spec(out_block),
        cost_estimate=pl.CostEstimate(flops=1_000_000, bytes_accessed=2_000_000, transcendentals=0),
        compiler_params=pltpu.CompilerParams(vmem_limit_bytes=24 * 1024 * 1024),
    )(operand)


def prepare_kernel(
    place_ref, lat_ref, ax_ref, obs_ref, obs_tiles, z_fwd, z_bwd, x_fwd, x_bwd, y_fwd, y_bwd, y_wide, rolled
):
    tile, side = place_ref[0], place_ref[1]
    for z in range(4):
        rolled[z] = pltpu.roll(obs_ref[z], place_ref[2], 1)

        def write(t, v, z=z):
            obs_tiles[PLACE[t], z] = v

        tiles_of(lambda rows, lanes, z=z: rolled[z, rows, lanes], write)
    band = pltpu.roll(ax_ref[...], 2 * NZ - G, 1)
    band = band / jnp.sum(band)
    wide = jnp.broadcast_to(band, (NZ, 2 * NZ))
    back = pltpu.roll(wide, 0, 1, stride=1, stride_axis=0)[:, :NZ]
    for m, ref in ((back.T, z_fwd), (back, z_bwd)):
        hi, lo = split(m)
        ref[pl.ds(0, NZ), pl.ds(0, NZ)] = hi
        ref[pl.ds(NZ, NZ), pl.ds(0, NZ)] = hi
        ref[pl.ds(0, NZ), pl.ds(NZ, NZ)] = lo
        ref[pl.ds(NZ, NZ), pl.ds(NZ, NZ)] = jnp.zeros_like(lo)
    total = lat_ref[0]
    for k in range(1, TAPS):
        total = total + lat_ref[k]
    for flip, outs, ins, ref in ((0, T, 2 * T, y_fwd), (1, T, 2 * T, y_bwd), (1, 2 * T, 3 * T, y_wide)):
        row = lax.broadcasted_iota(jnp.int32, (outs, 2 * NZ), 0)
        lane = lax.broadcasted_iota(jnp.int32, (outs, 2 * NZ), 1)
        high = lane < ins
        d = jnp.where(high, lane, lane - ins) - row - 1
        m = jnp.zeros((outs, 2 * NZ), F32)
        for k in range(TAPS):
            m = jnp.where(d == k, lat_ref[TAPS - 1 - k if flip else k], m)
        hi, lo = split(m)
        ref[pl.ds(0, outs), :] = hi[:, : 2 * ins]
        ref[pl.ds(outs, outs), :] = jnp.where(high, lo.astype(F32), 0.0).astype(BF16)[:, : 2 * ins]
    row = lax.broadcasted_iota(jnp.int32, (T, NZ), 0)
    lane = lax.broadcasted_iota(jnp.int32, (T, NZ), 1)
    own, first = lane < 64, (lane & 32) == 0
    col = lane & 31
    here = T * tile
    shifted = here + H * side
    wrap = lambda v: v & (NX - 1)
    src_f = wrap(jnp.where(own, here, here + T * side) + col)
    dst_f = wrap(shifted + row)
    src_b = wrap(jnp.where(own, shifted, shifted - T * side) + col)
    dst_b = wrap(here + row)
    for d, ref in ((src_f - dst_f, x_fwd), (dst_b - src_b, x_bwd)):
        m = jnp.zeros((T, NZ), F32)
        for k in range(TAPS):
            m = jnp.where(d == k - H, lat_ref[k], m)
        scale = jnp.full((T, NZ), total, F32)
        m = m / scale / scale
        hi, lo = split(m)
        ref[pl.ds(0, T), :] = hi
        ref[pl.ds(T, T), :] = jnp.where(first, lo.astype(F32), 0.0).astype(BF16)


def z_pass(v, m):
    r = jnp.dot(jnp.concatenate(split(v), axis=1), m, preferred_element_type=F32)
    return r[:, :NZ] + r[:, NZ:]


def x_pass(own, nbr, m):
    columns = []
    for o, n in zip(own, nbr):
        columns.append(jnp.concatenate([*split(o), *split(n)], axis=0))
    r = jnp.dot(m, jnp.concatenate(columns, axis=1), preferred_element_type=F32)
    r = r[:T] + r[T:]
    return [r[:, NZ * i : NZ * (i + 1)] for i in range(len(own))]


def y_pass(columns, m):
    outs = m.shape[0] // 2
    stacked = [jnp.concatenate(split(c), axis=0) for c in columns]
    r = jnp.dot(m, jnp.concatenate(stacked, axis=1), preferred_element_type=F32)
    return r[:outs] + r[outs:]


def part(ref, i, n):
    return ref[pl.ds(i * n, n), :]


def put_across(ref, i, v):
    ref[pl.ds(i, T, stride=T), :] = v


def in_order(tiles_ref, planes):
    for s in range(TILES):
        planes[pl.ds(32 * s, 32), :] = part(tiles_ref, PLACE[s], 32)


def arrive_xy_kernel(tiles_ref, out_ref, planes):
    in_order(tiles_ref, planes)
    for lo in range(8):
        v = planes[pl.ds(lo, NZ, stride=8), :].T
        for hi in range(4):
            put_across(out_ref, 8 * hi + lo, v[T * hi : T * (hi + 1)])


def arrive_yx_kernel(tiles_ref, out_ref, planes):
    in_order(tiles_ref, planes)
    for lo in range(8):
        v = planes[pl.ds(lo, NZ, stride=8), :].T
        for hi in range(4):
            out_ref[pl.ds(T * (8 * hi + lo), T), :] = v[T * hi : T * (hi + 1)]


def blur_kernel(my_ref, mz_ref, up, cur, down, out_ref):
    my, mz = my_ref[...], mz_ref[...]
    for x in range(0, T, 4):
        rows = []
        for i in (x, x + 2):
            columns = [
                jnp.concatenate([part(up, k, HALF), part(cur, k, T), part(down, k, HALF)], axis=0)
                for k in (i, i + 1)
            ]
            r = y_pass(columns, my)
            rows += [r[:, :NZ], r[:, NZ:]]
        w = z_pass(jnp.concatenate(rows, axis=0), mz)
        for i in range(4):
            put_across(out_ref, x + i, w[T * i : T * (i + 1)])


def quotient_kernel(m_ref, own_ref, nbr_ref, obs_ref, q_ref):
    m = m_ref[...]
    for y in range(0, T, 2):
        pair = (y, y + 1)
        blurred = x_pass([part(own_ref, k, T) for k in pair], [part(nbr_ref, k, T) for k in pair], m)
        for k, b in zip(pair, blurred):
            q_ref[pl.ds(k * T, T), :] = part(obs_ref, k, T) / b


def back_kernel(mx_ref, mz_ref, own_ref, nbr_ref, out_ref):
    mx, mz = mx_ref[...], mz_ref[...]
    for y in range(0, T, 4):
        rows = []
        for i in (y, y + 2):
            pair = (i, i + 1)
            rows += x_pass([part(own_ref, k, T) for k in pair], [part(nbr_ref, k, T) for k in pair], mx)
        w = z_pass(jnp.concatenate(rows, axis=0), mz)
        for i in range(4):
            put_across(out_ref, y + i, w[T * i : T * (i + 1)])


def update_kernel(
    back_ref, fwd_ref, mz_ref, up, own, down, cur_up, cur, cur_down, new_ref, out_ref
):
    back, fwd, mz = back_ref[...], fwd_ref[...], mz_ref[...]
    for x in range(0, T, 4):
        rows = []
        for i in (x, x + 2):
            pair = (i, i + 1)
            r = y_pass([jnp.concatenate([part(p, k, T) for p in (up, own, down)], axis=0) for k in pair], back)
            wide = []
            for n, k in enumerate(pair):
                old = jnp.concatenate(
                    [part(cur_up, k, HALF), part(cur, k, T), part(cur_down, k, HALF)], axis=0
                )
                new = old * r[:, NZ * n : NZ * (n + 1)]
                new_ref[pl.ds(k * T, T), :] = new[HALF : HALF + T]
                wide.append(new)
            r = y_pass(wide, fwd)
            rows += [r[:, :NZ], r[:, NZ:]]
        w = z_pass(jnp.concatenate(rows, axis=0), mz)
        for i in range(4):
            put_across(out_ref, x + i, w[T * i : T * (i + 1)])


def leave_kernel(m_ref, up, own, down, cur_ref, tiles_ref, work, planes):
    m = m_ref[...]
    for x in range(0, T, 2):
        pair = (x, x + 1)
        columns = [
            jnp.concatenate([part(up, k, HALF), part(own, k, T), part(down, k, HALF)], axis=0)
            for k in pair
        ]
        r = y_pass(columns, m)
        for n, k in enumerate(pair):
            work[pl.ds(k * T, T), :] = part(cur_ref, k, T) * r[:, NZ * n : NZ * (n + 1)]
    for lo in range(8):
        v = [work[pl.ds(8 * hi + lo, T, stride=T), :] for hi in range(4)]
        planes[pl.ds(lo, NZ, stride=8), :] = jnp.concatenate(v, axis=0).T
    for s in range(TILES):
        tiles_ref[pl.ds(32 * PLACE[s], 32), :] = part(planes, s, 32)


def local(observed, estimate, psf_lateral, psf_axial):
    n_z, n_y = lax.axis_size("gz"), lax.axis_size("gy")
    gz, gy = lax.axis_index("gz").astype(jnp.int32), lax.axis_index("gy").astype(jnp.int32)
    odd = gy % 2 == 1
    side = 1 - 2 * (gy % 2)
    joint = ("gz", "gy")

    def turn(sign):
        pairs = []
        for z in range(n_z):
            for y in range(n_y):
                s = sign * (1 if y % 2 == 0 else -1)
                pairs.append(((z + s) % n_z * n_y + y, z * n_y + y))
        return pairs

    ahead, behind = turn(1), turn(-1)
    outer = [p for i in range(1, n_y - 1, 2) for p in ((i, i + 1), (i + 1, i))]
    inner = [p for i in range(0, n_y, 2) for p in ((i, i + 1), (i + 1, i))]

    def y_swap(to_outer, to_inner):
        from_outer = lax.ppermute(to_outer, "gy", outer)
        from_inner = lax.ppermute(to_inner, "gy", inner)
        return jnp.where(odd, from_inner, from_outer), jnp.where(odd, from_outer, from_inner)

    def y_halves(v):
        v = v.reshape(T, T, NZ)
        first, second = v[:, :HALF], v[:, HALF:]
        swapped = y_swap(jnp.where(odd, second, first), jnp.where(odd, first, second))
        return [h.reshape(T * HALF, NZ) for h in swapped]

    def exchange(tiles):
        return lax.all_to_all(
            tiles, "gz", split_axis=0, concat_axis=0, tiled=True, axis_index_groups=[ORDER]
        )

    tiles_shape = (TILES, 4, 8, 128)
    flat = (NZ * 8, 128)
    block_shape = (4, T, NX)
    dma = lambda n: pltpu.SemaphoreType.DMA((n,))
    est_tiles = pl.pallas_call(
        depart_kernel,
        out_shape=jax.ShapeDtypeStruct(tiles_shape, F32),
        in_specs=[pl.BlockSpec(memory_space=pl.ANY)],
        out_specs=pl.BlockSpec(memory_space=pl.ANY),
        scratch_shapes=[pltpu.VMEM(block_shape, F32), pltpu.VMEM(tiles_shape, F32), dma(4), dma(4)],
        cost_estimate=pl.CostEstimate(flops=1_000_000, bytes_accessed=2_000_000, transcendentals=0),
        compiler_params=pltpu.CompilerParams(vmem_limit_bytes=60 * 1024 * 1024),
    )(estimate)
    place = jnp.stack([gz, side, jnp.where(odd, H, NX - H).astype(jnp.int32)])
    obs_tiles, z_fwd, z_bwd, x_fwd, x_bwd, y_fwd, y_bwd, y_wide = call(
        prepare_kernel,
        [(tiles_shape, F32)]
        + [((2 * NZ, 2 * NZ), BF16)] * 2
        + [((2 * T, 4 * T), BF16)] * 2
        + [((2 * T, 4 * T), BF16)] * 2
        + [((4 * T, 6 * T), BF16)],
        [place, psf_lateral, jnp.pad(psf_axial, (0, 2 * NZ - 2 * G - 1)).reshape(1, 2 * NZ), observed],
        smem=(0, 1),
        scratch=[pltpu.VMEM((4, T, NX), F32)],
    )
    est_tiles = exchange(est_tiles)
    obs_tiles = exchange(obs_tiles)
    whole = [(flat, F32)]
    planes = [pltpu.VMEM(flat, F32)]
    (current,) = call(arrive_xy_kernel, whole, [est_tiles.reshape(flat)], scratch=planes)
    (obs,) = call(arrive_yx_kernel, whole, [obs_tiles.reshape(flat)], scratch=planes)
    above, below = y_halves(current)
    (own,) = call(blur_kernel, whole, [y_fwd, z_fwd, above, current, below])
    for step in range(ITERS):
        (own,) = call(quotient_kernel, whole, [x_fwd, own, lax.ppermute(own, joint, ahead), obs])
        (own,) = call(back_kernel, whole, [x_bwd, z_bwd, own, lax.ppermute(own, joint, behind)])
        if step < ITERS - 1:
            up, down = y_swap(own, own)
            current, own = call(
                update_kernel,
                whole * 2,
                [y_wide, y_fwd, z_fwd, up, own, down, above, current, below],
            )
        else:
            up, down = y_halves(own)
            (tiles,) = call(
                leave_kernel, whole, [y_bwd, up, own, down, current], scratch=planes * 2
            )
    tiles = exchange(tiles.reshape(tiles_shape))
    tile_block = ((TILES, 1, 8, 128), 1)
    row_block = ((1, T, NX), 0)
    return per_plane(from_tiles_kernel, block_shape, tile_block, row_block, tiles)


def solution(mesh):
    in_specs = (P("gz", "gy", None), P("gz", "gy", None), P(), P())
    out_specs = P("gz", "gy", None)
    return jax.shard_map(local, mesh=mesh, in_specs=in_specs, out_specs=out_specs, check_vma=False)
```
